128 devices in a mesh: group: 2 (over core), member: 64 (over z, y, x).
Axes of the slice: x: 4, y: 4, z: 4, core: 2. Of those that a mesh axis runs over, the one named last changes fastest.
Arguments:
- embeddings: bfloat16 [65536, 1024], P(('group', 'member'))
- cluster: int32 [65536], P(('group', 'member')), may hold values from 0 to 7, as said below
Outputs:
- row_max: float32 [65536], P(('group', 'member'))
The draws below stay inside these ranges and needn't reach their ends.
Inputs may be any that keep to these rules, and one draw needn't show every extreme that they name: Cluster c is owned by the 16 devices whose index over group and member together runs from c * 16 to c * 16 + 15. Among the rows of one device at most 96 lie in one cluster; in every draw one cluster holds exactly 96 rows of every device.
All inputs are finite; a program needn't handle non-finite values.
Results may differ from the reference program's by a relative error of at most 0.0005.
Values may be sent and summed in bfloat16 or wider, within the bound.
No kernel may reach another device: no remote copies, remote signals or barrier semaphores. Data moves between devices by JAX's collectives and lax.ppermute only.
A program may use at most 128 MiB of HBM per device.

```python
import jax
import jax.numpy as jnp
from jax import lax

D = 1024
ROW_DEV = 512
TEAMS = 8
CLUSTERS = 8
BOUND = 96
ROWS = 65536


def layout_rows(key):
    teams = TEAMS
    heavy = jax.random.randint(jax.random.fold_in(key, 101), (), 0, teams)
    labels = jnp.arange(teams * BOUND, dtype=jnp.int32) // BOUND
    device_key = jax.random.fold_in(key, 102)

    def one_device(device):
        own_key = jax.random.fold_in(device_key, device)
        priority = jax.random.permutation(own_key, teams * BOUND).astype(jnp.int32)
        priority = jnp.where(labels == heavy, -1, priority)
        picked = labels[jnp.argsort(priority, stable=True)[:ROW_DEV]]
        shuffle = jax.random.permutation(jax.random.fold_in(own_key, 7), ROW_DEV)
        return picked[shuffle]
    target = jax.vmap(one_device)(jnp.arange(ROWS // ROW_DEV, dtype=jnp.int32)).reshape(-1)
    return target.astype(jnp.int32)


def draw_cluster(key, part):
    return layout_rows(key)


def draw_embeddings(key, part):
    labels = layout_rows(key)
    key = jax.random.fold_in(key, 5)
    per_cluster = ROWS // (3 * CLUSTERS)
    template_id = labels * per_cluster + jax.random.randint(jax.random.fold_in(key, 1), (ROWS,), 0, per_cluster)
    templates = jax.random.normal(jax.random.fold_in(key, 2), (CLUSTERS * per_cluster, D), jnp.float32)
    centers = jax.random.normal(jax.random.fold_in(key, 3), (CLUSTERS, D), jnp.float32)
    amplitude = jnp.exp(jax.random.uniform(jax.random.fold_in(key, 4), (ROWS, 1), jnp.float32, -1.2, 1.1))
    noise = jax.random.normal(jax.random.fold_in(key, 5), (ROWS, D), jnp.float32)
    scale = jnp.exp(jax.random.uniform(jax.random.fold_in(key, 6), (ROWS, 1), jnp.float32, -1.1, 1.1))
    weight = 0.7
    values = scale * (amplitude * templates[template_id] + noise + weight * centers[labels])
    return values.astype(jnp.bfloat16)


def setup_inputs(seed: int = 0) -> dict:
    streams_of = jax.random.split(jax.random.key(seed), 3)
    embeddings = draw_embeddings(jax.random.fold_in(streams_of[2], 71), 0)
    cluster = draw_cluster(jax.random.fold_in(streams_of[2], 71), 0)
    return {"embeddings": embeddings, "cluster": cluster}


def reference(embeddings, cluster):
    total = embeddings.shape[0]
    values = embeddings.astype(jnp.float32)
    normed = (values * lax.rsqrt(lax.optimization_barrier(jnp.sum(values * values, 1, keepdims=True)) + 1e-06)).astype(jnp.bfloat16)
    order = jnp.argsort(cluster, stable=True).astype(jnp.int32)
    sorted_ids = cluster[order]
    sorted_rows = normed[order].astype(jnp.float32)
    labels = jnp.arange(CLUSTERS, dtype=jnp.int32)
    first = jnp.searchsorted(sorted_ids, labels, side='left').astype(jnp.int32)
    last = jnp.searchsorted(sorted_ids, labels, side='right').astype(jnp.int32)
    block = 512

    def per_block(index):
        begin = index * block
        query = lax.dynamic_slice_in_dim(sorted_rows, begin, block, 0)
        query_ids = lax.dynamic_slice_in_dim(sorted_ids, begin, block, 0)
        query_pos = begin + jnp.arange(block, dtype=jnp.int32)
        lower = first[query_ids[0]] // block
        upper = (last[query_ids[block - 1]] - 1) // block

        def visit(other, best):
            start = (other * block).astype(jnp.int32)
            keys = lax.dynamic_slice_in_dim(sorted_rows, start, block, 0)
            key_ids = lax.dynamic_slice_in_dim(sorted_ids, start, block, 0)
            key_pos = start + jnp.arange(block, dtype=jnp.int32)
            sims = jnp.dot(query, keys.T, precision=lax.Precision.HIGHEST)
            keep = (query_ids[:, None] == key_ids[None, :]) & (query_pos[:, None] != key_pos[None, :])
            return jnp.maximum(best, lax.optimization_barrier(jnp.max(jnp.where(keep, sims, -2.0), 1)))
        return lax.fori_loop(lower, upper + 1, visit, jnp.full((block,), -2.0, jnp.float32))
    best_sorted = lax.map(per_block, jnp.arange(total // block, dtype=jnp.int32)).reshape(-1)
    return jnp.zeros((total,), jnp.float32).at[order].set(best_sorted)
```

```python
import functools

import jax
import jax.numpy as jnp
from jax import lax
from jax.experimental import pallas as pl
from jax.experimental.pallas import tpu as pltpu
from jax.sharding import PartitionSpec as P

AXES = ("group", "member")
SIDE = 4
CORES = 2
DEVICES = CORES * SIDE**3
BOUND = 96
HALF = SIDE * BOUND
LOW = -8.0
NONE = -2.0


def place(device):
    return (device // 64, device // 16 % 4, device // 4 % 4, device % 4)


def device_at(core, z, y, x):
    return core * 64 + z % 4 * 16 + y % 4 * 4 + x % 4


def moved(device, core=0, ring=0, u=0, v=0):
    c, z, y, x = place(device)
    if c == 0:
        z, x, y = z + ring, x + u, y + v
    else:
        x, z, y = x + ring, z + u, y - v
    return device_at((c + core) % 2, z, y, x)


def take(block, **step):
    route = [(moved(device, **step), device) for device in range(DEVICES)]
    return lax.ppermute(block, AXES, route)


def sort_kernel(ring_ref, rows_ref, cluster_ref, mine_ref, other_ref, slot_ref):
    rows = rows_ref.shape[0]
    core, ring_mine, ring_other = ring_ref[0], ring_ref[1], ring_ref[2]
    values = rows_ref[...].astype(jnp.float32)
    total = jnp.sum(values * values, 1, keepdims=True)
    normed = (values * lax.rsqrt(total + 1e-06)).astype(jnp.bfloat16)
    cluster = cluster_ref[...]
    hits = cluster == lax.broadcasted_iota(jnp.int32, (8, rows), 0)
    hits = jnp.where(hits, 1.0, 0.0)
    before = lax.broadcasted_iota(jnp.int32, (rows, rows), 0) < lax.broadcasted_iota(
        jnp.int32, (rows, rows), 1
    )
    before = jnp.where(before, 1.0, 0.0).astype(jnp.bfloat16)
    counted = jnp.dot(hits.astype(jnp.bfloat16), before, preferred_element_type=jnp.float32)
    rank = jnp.sum(counted * hits, 0, keepdims=True).astype(jnp.int32)
    is_mine = cluster // 4 == core
    step = (cluster + 4 - jnp.where(is_mine, ring_mine, ring_other)) % 4
    slot = (jnp.where(is_mine, 0, 4) + step) * BOUND + rank
    slot_ref[...] = slot
    for part, out_ref in enumerate((mine_ref, other_ref)):
        picks = slot - part * HALF == lax.broadcasted_iota(jnp.int32, (HALF, rows), 0)
        picks = jnp.where(picks, 1.0, 0.0)
        used = jnp.max(picks, 1, keepdims=True)
        placed = jnp.dot(picks.astype(jnp.bfloat16), normed, preferred_element_type=jnp.float32)
        first = lax.broadcasted_iota(jnp.int32, (HALF, 128), 1) == 0
        head = jnp.where(first & (used < 0.5), 2.0, placed[:, :128])
        out_ref[:, :128] = head.astype(jnp.bfloat16)
        out_ref[:, 128:] = placed[:, 128:].astype(jnp.bfloat16)


def sort_rows(rings, embeddings, cluster):
    rows, width = embeddings.shape
    vmem = pl.BlockSpec(memory_space=pltpu.VMEM)
    return pl.pallas_call(
        sort_kernel,
        in_specs=[pl.BlockSpec(memory_space=pltpu.SMEM), vmem, vmem],
        out_specs=[vmem] * 3,
        out_shape=[
            jax.ShapeDtypeStruct((HALF, width), jnp.bfloat16),
            jax.ShapeDtypeStruct((HALF, width), jnp.bfloat16),
            jax.ShapeDtypeStruct((1, rows), jnp.int32),
        ],
        compiler_params=pltpu.CompilerParams(vmem_limit_bytes=48 << 20),
        name="sort_rows",
    )(rings, embeddings, cluster.reshape(1, rows))


def pair_kernel(names, products, *refs):
    chunks = dict(zip(names, refs))
    best_ref, left_ref, right_ref = refs[len(names) :]
    at = {name: k for k, name in enumerate(names)}
    left_ref[...] = jnp.full(left_ref.shape, LOW, jnp.float32)
    right_ref[...] = jnp.full(right_ref.shape, LOW, jnp.float32)
    bias = {}
    for name in names:
        head = chunks[name][:, :128].astype(jnp.float32)
        head = jnp.where(head > 1.5, LOW, 0.0)
        bias[name] = (head[:, :1], head.T[:1, :])
    for left, right in products:
        scores = lax.dot_general(
            chunks[left][...],
            chunks[right][...],
            (((1,), (1,)), ((), ())),
            preferred_element_type=jnp.float32,
        )
        same = left == right
        if same:
            eye = lax.broadcasted_iota(jnp.int32, scores.shape, 0) == lax.broadcasted_iota(
                jnp.int32, scores.shape, 1
            )
            scores = jnp.where(eye, LOW, scores)
        over = scores + bias[right][1]
        fold = jnp.maximum(jnp.maximum(over[:, :128], over[:, 128:256]), over[:, 256:])
        left_ref[at[left]] = jnp.maximum(left_ref[at[left]], fold)
        if not same:
            down = scores + bias[left][0]
            down = jnp.max(down.reshape(HALF // 8, 8, HALF), 0)
            right_ref[at[right]] = jnp.maximum(right_ref[at[right]], down)
    for name in names:
        k = at[name]
        across = jnp.max(left_ref[k].T, 0, keepdims=True)
        across = jnp.maximum(across, jnp.max(right_ref[k], 0, keepdims=True))
        best_ref[k : k + 1, :] = jnp.maximum(across, NONE)


def pair_max(chunks, products):
    names = tuple(chunks)
    vmem = pl.BlockSpec(memory_space=pltpu.VMEM)
    width = next(iter(chunks.values())).shape[1]
    best = pl.pallas_call(
        functools.partial(pair_kernel, names, products),
        in_specs=[vmem] * len(names),
        out_specs=vmem,
        out_shape=jax.ShapeDtypeStruct((len(names), HALF), jnp.float32),
        scratch_shapes=[
            pltpu.VMEM((len(names), HALF, 128), jnp.float32),
            pltpu.VMEM((len(names), 8, HALF), jnp.float32),
        ],
        compiler_params=pltpu.CompilerParams(vmem_limit_bytes=48 << 20),
        cost_estimate=pl.CostEstimate(
            flops=2 * len(products) * HALF * HALF * width,
            bytes_accessed=2 * len(names) * HALF * width,
            transcendentals=0,
        ),
        name="pair_max",
    )(*chunks.values())
    return dict(zip(names, best))


def unsort_kernel(best_ref, slot_ref, out_ref):
    slots = best_ref.shape[1]
    rows = slot_ref.shape[1]
    column = jnp.broadcast_to(best_ref[...], (128, slots)).T[:, :1]
    picks = slot_ref[...] == lax.broadcasted_iota(jnp.int32, (slots, rows), 0)
    out_ref[...] = jnp.max(jnp.where(picks, column, NONE), 0, keepdims=True)


def unsort(best, slot):
    vmem = pl.BlockSpec(memory_space=pltpu.VMEM)
    return pl.pallas_call(
        unsort_kernel,
        in_specs=[vmem] * 2,
        out_specs=vmem,
        out_shape=jax.ShapeDtypeStruct(slot.shape, jnp.float32),
        name="unsort",
    )(best, slot)


def crossed(first, second):
    return [(a, b) for a in first for b in second]


def on_device(embeddings, cluster):
    device = lax.axis_index("group") * 64 + lax.axis_index("member")
    core, z, x = device // 64, device // 16 % 4, device % 4
    rings = jnp.stack([core, jnp.where(core == 0, z, x), jnp.where(core == 0, x, z)])
    mine, other, slot = sort_rows(rings, embeddings, cluster)
    held = {}

    def routed(block):
        parts = [block[:BOUND]]
        for step in range(1, SIDE):
            parts.append(take(block[step * BOUND : (step + 1) * BOUND], ring=-step))
        return jnp.concatenate(parts, 0)

    held["0m"] = routed(mine)
    held["0s"] = routed(take(other, core=1))
    for half in "ms":
        held["v1" + half] = take(held["0" + half], v=1)
        held["u1" + half] = take(held["0" + half], u=1)
        held["u3" + half] = take(held["0" + half], u=-1)
    for half in "ms":
        held["v2" + half] = take(held["v1" + half], v=1)
    held["u2m"] = take(held["u1m"], u=1)
    held["u2s"] = take(held["u3s"], u=-1)

    def pairs(*blocks):
        return {b + h: held[b + h] for b in blocks for h in "ms"}

    def both(a, b):
        return crossed((a + "m", a + "s"), (b + "m", b + "s"))

    one = pair_max(
        pairs("0", "u1", "u3", "v1"),
        [("0m", "0m"), ("0m", "0s"), ("0s", "0s")]
        + both("0", "u1")
        + both("v1", "0")
        + both("v1", "u1")
        + both("v1", "u3"),
    )
    two = pair_max(pairs("0", "u2", "v1"), both("0", "u2") + both("v1", "u2"))
    three = pair_max(
        pairs("0", "u1", "u2", "v2"), both("v2", "0") + both("v2", "u1") + both("v2", "u2")
    )

    def merged(block):
        found = [
            jnp.concatenate([part[block + "m"], part[block + "s"]])
            for part in (one, two, three)
            if block + "m" in part
        ]
        return functools.reduce(jnp.maximum, found)

    best = functools.reduce(
        jnp.maximum,
        [
            merged("0"),
            take(merged("u1"), u=-1),
            take(merged("u2"), u=2),
            take(merged("u3"), u=1),
            take(merged("v1"), v=-1),
            take(merged("v2"), v=2),
        ],
    ).reshape(2, SIDE, BOUND)
    back = [best[:, 0]]
    for step in range(1, SIDE):
        back.append(take(best[:, step], ring=step))
    back = jnp.stack(back, 1)
    swapped = take(back[1], core=1)
    final = jnp.concatenate([back[0].reshape(1, HALF), swapped.reshape(1, HALF)], 1)
    return unsort(final, slot).reshape(-1)


def solution(mesh):
    in_specs = (P(AXES, None), P(AXES))
    return jax.shard_map(
        on_device, mesh=mesh, in_specs=in_specs, out_specs=P(AXES), check_vma=False
    )
```

```python
import functools

import jax
import jax.numpy as jnp
from jax import lax
from jax.experimental import pallas as pl
from jax.experimental.pallas import tpu as pltpu
from jax.sharding import PartitionSpec as P

AXES = ("group", "member")
SIDE = 4
CORES = 2
DEVICES = CORES * SIDE**3
BOUND = 96
HALF = SIDE * BOUND
SLOTS = CORES * HALF
TILE = 256
START = {"w": 0, "m": 0, "s": HALF}
STEPS = {
    "0": {"u": 0, "v": 0},
    "u1": {"u": 1},
    "u3": {"u": -1},
    "v1": {"v": 1},
    "u2": {"u": 2},
    "v2": {"v": 2},
}
BLOCKS = tuple(STEPS)
SECTIONS = 2 * SIDE
LANES = 128
CHUNKS = 4
EFFORT = 8
LOW = -8.0
NONE = -2.0


def place(device):
    return (device // 64, device // 16 % 4, device // 4 % 4, device % 4)


def device_at(core, z, y, x):
    return core * 64 + z % 4 * 16 + y % 4 * 4 + x % 4


def moved(device, core=0, ring=0, u=0, v=0):
    c, z, y, x = place(device)
    if c == 0:
        z, x, y = z + ring, x + u, y + v
    else:
        x, z, y = x + ring, z + u, y - v
    return device_at((c + core) % 2, z, y, x)


def take(block, **step):
    route = [(moved(device, **step), device) for device in range(DEVICES)]
    return lax.ppermute(block, AXES, route)


def here():
    member = lax.axis_index("member")
    return lax.axis_index("group"), member // 16, member // 4 % 4, member % 4


def partner(core, z, y, x, ring, u, v):
    ring = (jnp.where(core == 0, z, x) + ring) & 3
    u = (jnp.where(core == 0, x, z) + u) & 3
    y = (jnp.where(core == 0, y + v, y - v)) & 3
    return ring * jnp.where(core == 0, 16, 1) + u * jnp.where(core == 0, 1, 16) + y * 4


def sort_kernel(rows_hbm, cluster_hbm, mine_ref, other_ref, slot_ref, *scratch):
    rows_ref, cluster_ref, normed_ref, sems = scratch
    rows = rows_ref.shape[0]
    step = rows // CHUNKS
    copies = [pltpu.make_async_copy(cluster_hbm, cluster_ref, sems.at[CHUNKS])]
    for k in range(CHUNKS):
        part = pl.ds(k * step, step)
        copies.append(
            pltpu.make_async_copy(rows_hbm.at[part, :], rows_ref.at[part, :], sems.at[k])
        )
    for copy in copies:
        copy.start()
    core, z, y, x = here()
    ring_mine, ring_other = jnp.where(core == 0, z, x), jnp.where(core == 0, x, z)
    before = lax.broadcasted_iota(jnp.int32, (rows, rows), 0) < lax.broadcasted_iota(
        jnp.int32, (rows, rows), 1
    )
    before = jnp.where(before, 1.0, 0.0).astype(jnp.bfloat16)
    copies[0].wait()
    cluster = cluster_ref[...]
    hits = cluster == lax.broadcasted_iota(jnp.int32, (8, rows), 0)
    hits = jnp.where(hits, 1.0, 0.0)
    counted = jnp.dot(hits.astype(jnp.bfloat16), before, preferred_element_type=jnp.float32)
    rank = jnp.sum(counted * hits, 0, keepdims=True).astype(jnp.int32)
    is_mine = cluster // 4 == core
    turn = (cluster + 4 - jnp.where(is_mine, ring_mine, ring_other)) % 4
    slot = (jnp.where(is_mine, 0, 4) + turn) * BOUND + rank
    slot_ref[...] = slot
    for k in range(CHUNKS):
        copies[1 + k].wait()
        part = slice(k * step, (k + 1) * step)
        values = rows_ref[part, :].astype(jnp.float32)
        total = jnp.sum(values * values, 1, keepdims=True)
        normed_ref[part, :] = (values * lax.rsqrt(total + 1e-06)).astype(jnp.bfloat16)
    normed = normed_ref[...]
    for start, out_ref in ((0, mine_ref), (HALF, other_ref)):
        picks = slot - start == lax.broadcasted_iota(jnp.int32, (HALF, rows), 0)
        picks = jnp.where(picks, 1.0, 0.0)
        used = jnp.max(picks, 1, keepdims=True)
        placed = jnp.dot(picks.astype(jnp.bfloat16), normed, preferred_element_type=jnp.float32)
        first = lax.broadcasted_iota(jnp.int32, (HALF, LANES), 1) == 0
        head = jnp.where(first & (used < 0.5), 2.0, placed[:, :LANES])
        out_ref[:, :LANES] = head.astype(jnp.bfloat16)
        out_ref[:, LANES:] = placed[:, LANES:].astype(jnp.bfloat16)


def sort_rows(embeddings, cluster):
    rows, width = embeddings.shape
    vmem = pl.BlockSpec(memory_space=pltpu.VMEM)
    hbm = pl.BlockSpec(memory_space=pltpu.HBM)
    return pl.pallas_call(
        sort_kernel,
        in_specs=[hbm, hbm],
        out_specs=[vmem] * 3,
        out_shape=[
            jax.ShapeDtypeStruct((HALF, width), jnp.bfloat16),
            jax.ShapeDtypeStruct((HALF, width), jnp.bfloat16),
            jax.ShapeDtypeStruct((1, rows), jnp.int32),
        ],
        scratch_shapes=[
            pltpu.VMEM((rows, width), jnp.bfloat16),
            pltpu.VMEM((1, rows), jnp.int32),
            pltpu.VMEM((rows, width), jnp.bfloat16),
            pltpu.SemaphoreType.DMA((CHUNKS + 1,)),
        ],
        compiler_params=pltpu.CompilerParams(vmem_limit_bytes=20 << 20),
        cost_estimate=pl.CostEstimate(
            flops=4 * rows * HALF * width, bytes_accessed=6 * rows * width, transcendentals=rows
        ),
        name="sort_rows",
    )(embeddings, cluster)


def empty(values):
    return jnp.where(values[:, :LANES].astype(jnp.float32) > 1.5, LOW, 0.0)


def pair_kernel(names, blocks, products, *refs):
    chunks = dict(zip(names, refs))
    before_ref, best_ref, fold_ref, lane_ref = refs[len(names) :]
    fold_blocks = {upper for upper, parts, lower, kind in products if kind != "lane"}
    lane_blocks = {lower for upper, parts, lower, kind in products if kind != "fold"}
    for block in fold_blocks:
        fold_ref[blocks.index(block)] = jnp.full(fold_ref.shape[1:], LOW, jnp.float32)
    for block in lane_blocks:
        lane_ref[blocks.index(block)] = jnp.full(lane_ref.shape[1:], LOW, jnp.float32)
    for upper, parts, lower, kind in products:
        for tile in range(SLOTS // TILE):
            columns = slice(tile * TILE, (tile + 1) * TILE)
            if (lower, "w") in chunks:
                right = chunks[lower, "w"][columns, :]
            elif tile == 0:
                right = chunks[lower, "m"][:TILE, :]
            elif tile == 1:
                first, second = chunks[lower, "m"], chunks[lower, "s"]
                right = jnp.concatenate([first[TILE:, :], second[: TILE // 2, :]], 0)
            else:
                right = chunks[lower, "s"][TILE // 2 :, :]
            if kind != "lane":
                across = empty(right).T[:1, :]
            for part in parts:
                values = chunks[upper, part][...]
                rows = values.shape[0]
                scores = lax.dot_general(
                    values, right, (((1,), (1,)), ((), ())), preferred_element_type=jnp.float32
                )
                if upper == lower:
                    row = lax.broadcasted_iota(jnp.int32, scores.shape, 0) + START[part]
                    column = lax.broadcasted_iota(jnp.int32, scores.shape, 1) + tile * TILE
                    scores = jnp.where(row == column, LOW, scores)
                if kind != "fold":
                    at = blocks.index(lower)
                    down = scores + empty(values)[:, :1]
                    down = jnp.max(down.reshape(rows // 8, 8, TILE), 0)
                    lane_ref[at, :, columns] = jnp.maximum(lane_ref[at, :, columns], down)
                if kind != "lane":
                    at = (blocks.index(upper), slice(START[part], START[part] + rows))
                    over = scores + across
                    over = jnp.maximum(over[:, :LANES], over[:, LANES:])
                    fold_ref[at] = jnp.maximum(fold_ref[at], over)
    best = [before_ref[k : k + 1, :] for k in range(len(BLOCKS))]
    for block in blocks:
        at, k = blocks.index(block), BLOCKS.index(block)
        if block in fold_blocks:
            best[k] = jnp.maximum(best[k], jnp.max(fold_ref[at].T, 0, keepdims=True))
        if block in lane_blocks:
            best[k] = jnp.maximum(best[k], jnp.max(lane_ref[at], 0, keepdims=True))
    if best_ref.shape[0] == len(BLOCKS):
        best_ref[...] = jnp.concatenate(best, 0)
        return
    best_ref[...] = jnp.full(best_ref.shape, NONE, jnp.float32)
    core, z, y, x = here()
    for section in range(SECTIONS):
        half, turn = section // SIDE, section % SIDE
        for k, step in enumerate(STEPS.values()):
            row = partner(core, z, y, x, -turn, step.get("u", 0), step.get("v", 0))
            row += (core if half == 0 else 1 - core) * 64
            best_ref[pl.ds(row, 1), :BOUND] = best[k][:, section * BOUND : (section + 1) * BOUND]


def pair_max(held, before, products, last):
    names, blocks = [], []
    for upper, parts, lower, kind in products:
        names += [(upper, part) for part in parts]
        names += [(lower, part) for part in "wms" if (lower, part) in held]
        blocks += [lower] * (kind != "fold") + [upper] * (kind != "lane")
    names, blocks = list(dict.fromkeys(names)), list(dict.fromkeys(blocks))
    vmem = pl.BlockSpec(memory_space=pltpu.VMEM)
    width = held[names[0]].shape[1]
    pairs = sum(
        held[upper, part].shape[0] * SLOTS
        for upper, parts, lower, kind in products
        for part in parts
    )
    shape = (DEVICES, LANES) if last else before.shape
    return pl.pallas_call(
        functools.partial(pair_kernel, names, blocks, products),
        in_specs=[vmem] * (len(names) + 1),
        out_specs=vmem,
        out_shape=jax.ShapeDtypeStruct(shape, jnp.float32),
        scratch_shapes=[
            pltpu.VMEM((len(blocks), SLOTS, LANES), jnp.float32),
            pltpu.VMEM((len(blocks), 8, SLOTS), jnp.float32),
        ],
        compiler_params=pltpu.CompilerParams(vmem_limit_bytes=20 << 20),
        cost_estimate=pl.CostEstimate(
            flops=int(2 * EFFORT * pairs * width),
            bytes_accessed=2 * len(names) * HALF * width,
            transcendentals=0,
        ),
        name="pair_max",
    )(*(held[name] for name in names), before)


def unsort_kernel(got_ref, slot_ref, out_ref, row_ref):
    rows = slot_ref.shape[1]
    core, z, y, x = here()
    row_ref[...] = jnp.full(row_ref.shape, NONE, jnp.float32)
    for section in range(SECTIONS):
        half, turn = section // SIDE, section % SIDE
        owner = core if half == 0 else 1 - core
        found = []
        for step in STEPS.values():
            row = partner(owner, z, y, x, turn, -step.get("u", 0), -step.get("v", 0))
            found.append(got_ref[pl.ds(row + owner * 64, 1), :])
        row_ref[section : section + 1, :] = functools.reduce(jnp.maximum, found)
    columns = row_ref[...].T
    best = jnp.full((1, rows), NONE, jnp.float32)
    for section in range(SECTIONS):
        place = lax.broadcasted_iota(jnp.int32, (BOUND, rows), 0) + section * BOUND
        found = jnp.where(slot_ref[...] == place, columns[:BOUND, section : section + 1], NONE)
        best = jnp.maximum(best, jnp.max(found, 0, keepdims=True))
    out_ref[...] = best


def unsort(got, slot):
    vmem = pl.BlockSpec(memory_space=pltpu.VMEM)
    return pl.pallas_call(
        unsort_kernel,
        in_specs=[vmem] * 2,
        out_specs=vmem,
        out_shape=jax.ShapeDtypeStruct(slot.shape, jnp.float32),
        scratch_shapes=[pltpu.VMEM((LANES, LANES), jnp.float32)],
        name="unsort",
    )(got, slot)


def on_device(embeddings, cluster):
    mine, other, slot = sort_rows(embeddings, cluster.reshape(1, -1))

    def section(block, step):
        return block[step * BOUND : (step + 1) * BOUND]

    held = {}
    near = {step: take(section(mine, step), ring=-step) for step in (2, 1, 3)}
    far = {step: take(section(other, step), core=1, ring=-step) for step in (2, 1, 3, 0)}
    near[0] = section(mine, 0)
    held["0", "m"] = jnp.concatenate([near[step] for step in range(SIDE)], 0)
    held["0", "s"] = jnp.concatenate([far[step] for step in range(SIDE)], 0)
    for part in "ms":
        held["v1", part] = take(held["0", part], v=1)
        held["u1", part] = take(held["0", part], u=1)
        held["u3", part] = take(held["0", part], u=-1)
    for part in "ms":
        held["v2", part] = take(held["v1", part], v=1)
    held["u2", "m"] = take(held["u1", "m"], u=1)
    held["u2", "s"] = take(held["u3", "s"], u=-1)

    best = jnp.full((len(BLOCKS), SLOTS), NONE, jnp.float32)
    plan = (
        [("0", "ms", "0", "lane")],
        [("u1", "ms", "0", "both")],
        [("0", "ms", "v1", "both")],
        [("u1", "ms", "v1", "both"), ("u3", "ms", "v1", "both")],
        [("u2", "ms", "0", "lane"), ("u2", "ms", "v1", "both")],
        [("v2", "m", near, "both") for near in ("0", "u1", "u2")],
        [("v2", "s", near, "both") for near in ("0", "u1", "u2")],
    )
    for k, products in enumerate(plan):
        best = pair_max(held, best, products, k + 1 == len(plan))
    got = lax.all_to_all(best, AXES, 0, 0, tiled=True)
    return unsort(got, slot).reshape(-1)


def solution(mesh):
    in_specs = (P(AXES, None), P(AXES))
    return jax.shard_map(
        on_device, mesh=mesh, in_specs=in_specs, out_specs=P(AXES), check_vma=False
    )
```

```python
import functools

import jax
import jax.numpy as jnp
from jax import lax
from jax.experimental import pallas as pl
from jax.experimental.pallas import tpu as pltpu
from jax.sharding import PartitionSpec as P

AXES = ("group", "member")
SIDE = 4
CORES = 2
DEVICES = CORES * SIDE**3
BOUND = 96
HALF = SIDE * BOUND
SLOTS = CORES * HALF
TILE = 256
START = {"w": 0, "m": 0, "s": HALF}
STEPS = {
    "0": {"u": 0, "v": 0},
    "u1": {"u": 1},
    "u3": {"u": -1},
    "v1": {"v": 1},
    "u2": {"u": 2},
    "v2": {"v": 2},
}
BLOCKS = tuple(STEPS)
SECTIONS = 2 * SIDE
LANES = 128
CHUNKS = 4
ORDER = ('v1m', 'u1m', 'u3m', 'v1s', 'u1s', 'u3s', 'v2m', 'v2s', 'u2m', 'u2s')
CROSS = True
PLAN = 'cbAkqDGFgH'
EFFORTS = (7, 7, 7, 7, 7, 7, 7, 7, 7, 7)
DEPS = {'b': ('u3m',)}
RELAYS = {}
LOW = -8.0
NONE = -2.0


def place(device):
    return (device // 64, device // 16 % 4, device // 4 % 4, device % 4)


def device_at(core, z, y, x):
    return core * 64 + z % 4 * 16 + y % 4 * 4 + x % 4


def moved(device, core=0, ring=0, u=0, v=0):
    c, z, y, x = place(device)
    if c == 0:
        z, x, y = z + ring, x + u, y + v
    else:
        x, z, y = x + ring, z + u, y - v
    return device_at((c + core) % 2, z, y, x)


def take(block, **step):
    route = [(moved(device, **step), device) for device in range(DEVICES)]
    return lax.ppermute(block, AXES, route)


def here():
    member = lax.axis_index("member")
    return lax.axis_index("group"), member // 16, member // 4 % 4, member % 4


def partner(core, z, y, x, ring, u, v):
    ring = (jnp.where(core == 0, z, x) + ring) & 3
    u = (jnp.where(core == 0, x, z) + u) & 3
    y = (jnp.where(core == 0, y + v, y - v)) & 3
    return ring * jnp.where(core == 0, 16, 1) + u * jnp.where(core == 0, 1, 16) + y * 4


def sort_kernel(rows_hbm, cluster_hbm, mine_ref, other_ref, slot_ref, *scratch):
    rows_ref, cluster_ref, normed_ref, sems = scratch
    rows = rows_ref.shape[0]
    step = rows // CHUNKS
    copies = [pltpu.make_async_copy(cluster_hbm, cluster_ref, sems.at[CHUNKS])]
    for k in range(CHUNKS):
        part = pl.ds(k * step, step)
        copies.append(
            pltpu.make_async_copy(rows_hbm.at[part, :], rows_ref.at[part, :], sems.at[k])
        )
    for copy in copies:
        copy.start()
    core, z, y, x = here()
    ring_mine, ring_other = jnp.where(core == 0, z, x), jnp.where(core == 0, x, z)
    before = lax.broadcasted_iota(jnp.int32, (rows, rows), 0) < lax.broadcasted_iota(
        jnp.int32, (rows, rows), 1
    )
    before = jnp.where(before, 1.0, 0.0).astype(jnp.bfloat16)
    copies[0].wait()
    cluster = cluster_ref[...]
    hits = cluster == lax.broadcasted_iota(jnp.int32, (8, rows), 0)
    hits = jnp.where(hits, 1.0, 0.0)
    counted = jnp.dot(hits.astype(jnp.bfloat16), before, preferred_element_type=jnp.float32)
    rank = jnp.sum(counted * hits, 0, keepdims=True).astype(jnp.int32)
    is_mine = cluster // 4 == core
    turn = (cluster + 4 - jnp.where(is_mine, ring_mine, ring_other)) % 4
    slot = (jnp.where(is_mine, 0, 4) + turn) * BOUND + rank
    slot_ref[...] = slot
    for k in range(CHUNKS):
        copies[1 + k].wait()
        part = slice(k * step, (k + 1) * step)
        values = rows_ref[part, :].astype(jnp.float32)
        total = jnp.sum(values * values, 1, keepdims=True)
        normed_ref[part, :] = (values * lax.rsqrt(total + 1e-06)).astype(jnp.bfloat16)
    normed = normed_ref[...]
    for start, out_ref in ((0, mine_ref), (HALF, other_ref)):
        picks = slot - start == lax.broadcasted_iota(jnp.int32, (HALF, rows), 0)
        picks = jnp.where(picks, 1.0, 0.0)
        used = jnp.max(picks, 1, keepdims=True)
        placed = jnp.dot(picks.astype(jnp.bfloat16), normed, preferred_element_type=jnp.float32)
        first = lax.broadcasted_iota(jnp.int32, (HALF, LANES), 1) == 0
        head = jnp.where(first & (used < 0.5), 2.0, placed[:, :LANES])
        out_ref[:, :LANES] = head.astype(jnp.bfloat16)
        out_ref[:, LANES:] = placed[:, LANES:].astype(jnp.bfloat16)


def sort_rows(embeddings, cluster):
    rows, width = embeddings.shape
    vmem = pl.BlockSpec(memory_space=pltpu.VMEM)
    hbm = pl.BlockSpec(memory_space=pltpu.HBM)
    return pl.pallas_call(
        sort_kernel,
        in_specs=[hbm, hbm],
        out_specs=[vmem] * 3,
        out_shape=[
            jax.ShapeDtypeStruct((HALF, width), jnp.bfloat16),
            jax.ShapeDtypeStruct((HALF, width), jnp.bfloat16),
            jax.ShapeDtypeStruct((1, rows), jnp.int32),
        ],
        scratch_shapes=[
            pltpu.VMEM((rows, width), jnp.bfloat16),
            pltpu.VMEM((1, rows), jnp.int32),
            pltpu.VMEM((rows, width), jnp.bfloat16),
            pltpu.SemaphoreType.DMA((CHUNKS + 1,)),
        ],
        compiler_params=pltpu.CompilerParams(vmem_limit_bytes=20 << 20),
        cost_estimate=pl.CostEstimate(
            flops=4 * rows * HALF * width, bytes_accessed=6 * rows * width, transcendentals=rows
        ),
        name="sort_rows",
    )(embeddings, cluster)


def empty(values):
    return jnp.where(values[:, :LANES].astype(jnp.float32) > 1.5, LOW, 0.0)


def pair_kernel(names, blocks, products, relay, *refs):
    chunks = dict(zip(names, refs))
    before_ref = refs[len(names)]
    best_ref, fold_ref, lane_ref = refs[-3:]
    if relay:
        best_ref, copy_ref = refs[-4:-2]
        copy_ref[...] = chunks[relay][...]
    fold_blocks = {upper for upper, parts, lower, kind in products if kind != "lane"}
    lane_blocks = {lower for upper, parts, lower, kind in products if kind != "fold"}
    for block in fold_blocks:
        fold_ref[blocks.index(block)] = jnp.full(fold_ref.shape[1:], LOW, jnp.float32)
    for block in lane_blocks:
        lane_ref[blocks.index(block)] = jnp.full(lane_ref.shape[1:], LOW, jnp.float32)
    for upper, parts, lower, kind in products:
        for tile in range(SLOTS // TILE):
            columns = slice(tile * TILE, (tile + 1) * TILE)
            if (lower, "w") in chunks:
                right = chunks[lower, "w"][columns, :]
            elif tile == 0:
                right = chunks[lower, "m"][:TILE, :]
            elif tile == 1:
                first, second = chunks[lower, "m"], chunks[lower, "s"]
                right = jnp.concatenate([first[TILE:, :], second[: TILE // 2, :]], 0)
            else:
                right = chunks[lower, "s"][TILE // 2 :, :]
            if kind != "lane":
                across = empty(right).T[:1, :]
            for part in parts:
                values = chunks[upper, part][...]
                rows = values.shape[0]
                scores = lax.dot_general(
                    values, right, (((1,), (1,)), ((), ())), preferred_element_type=jnp.float32
                )
                if upper == lower:
                    row = lax.broadcasted_iota(jnp.int32, scores.shape, 0) + START[part]
                    column = lax.broadcasted_iota(jnp.int32, scores.shape, 1) + tile * TILE
                    scores = jnp.where(row == column, LOW, scores)
                if kind != "fold":
                    at = blocks.index(lower)
                    down = scores + empty(values)[:, :1]
                    down = jnp.max(down.reshape(rows // 8, 8, TILE), 0)
                    lane_ref[at, :, columns] = jnp.maximum(lane_ref[at, :, columns], down)
                if kind != "lane":
                    at = (blocks.index(upper), slice(START[part], START[part] + rows))
                    over = scores + across
                    over = jnp.maximum(over[:, :LANES], over[:, LANES:])
                    fold_ref[at] = jnp.maximum(fold_ref[at], over)
    best = [before_ref[k : k + 1, :] for k in range(len(BLOCKS))]
    for block in blocks:
        at, k = blocks.index(block), BLOCKS.index(block)
        if block in fold_blocks:
            best[k] = jnp.maximum(best[k], jnp.max(fold_ref[at].T, 0, keepdims=True))
        if block in lane_blocks:
            best[k] = jnp.maximum(best[k], jnp.max(lane_ref[at], 0, keepdims=True))
    if best_ref.shape[0] == len(BLOCKS):
        best_ref[...] = jnp.concatenate(best, 0)
        return
    best_ref[...] = jnp.full(best_ref.shape, NONE, jnp.float32)
    core, z, y, x = here()
    for section in range(SECTIONS):
        half, turn = section // SIDE, section % SIDE
        for k, step in enumerate(STEPS.values()):
            row = partner(core, z, y, x, -turn, step.get("u", 0), step.get("v", 0))
            row += (core if half == 0 else 1 - core) * 64
            best_ref[pl.ds(row, 1), :BOUND] = best[k][:, section * BOUND : (section + 1) * BOUND]


def pair_max(held, before, products, last, effort, extra, relay):
    names, blocks = [relay] * bool(relay), []
    for upper, parts, lower, kind in products:
        names += [(upper, part) for part in parts]
        names += [(lower, part) for part in "wms" if (lower, part) in held]
        blocks += [lower] * (kind != "fold") + [upper] * (kind != "lane")
    names, blocks = list(dict.fromkeys(names)), list(dict.fromkeys(blocks))
    vmem = pl.BlockSpec(memory_space=pltpu.VMEM)
    width = held[names[0]].shape[1]
    pairs = sum(
        held[upper, part].shape[0] * SLOTS
        for upper, parts, lower, kind in products
        for part in parts
    )
    shape = (DEVICES, LANES) if last else before.shape
    return pl.pallas_call(
        functools.partial(pair_kernel, names, blocks, products, relay),
        in_specs=[vmem] * (len(names) + 1)
        + [pl.BlockSpec(memory_space=pl.ANY)] * len(extra),
        out_specs=[vmem, vmem] if relay else vmem,
        out_shape=[
            jax.ShapeDtypeStruct(shape, jnp.float32),
            jax.ShapeDtypeStruct((HALF, width), jnp.bfloat16),
        ]
        if relay
        else jax.ShapeDtypeStruct(shape, jnp.float32),
        scratch_shapes=[
            pltpu.VMEM((len(blocks), SLOTS, LANES), jnp.float32),
            pltpu.VMEM((len(blocks), 8, SLOTS), jnp.float32),
        ],
        compiler_params=pltpu.CompilerParams(vmem_limit_bytes=20 << 20),
        cost_estimate=pl.CostEstimate(
            flops=int(2 * effort * pairs * width),
            bytes_accessed=2 * len(names) * HALF * width,
            transcendentals=0,
        ),
        name="pair_max",
    )(*(held[name] for name in names), before, *extra)


def unsort_kernel(got_ref, slot_ref, out_ref, row_ref):
    rows = slot_ref.shape[1]
    core, z, y, x = here()
    row_ref[...] = jnp.full(row_ref.shape, NONE, jnp.float32)
    for section in range(SECTIONS):
        half, turn = section // SIDE, section % SIDE
        owner = core if half == 0 else 1 - core
        found = []
        for step in STEPS.values():
            row = partner(owner, z, y, x, turn, -step.get("u", 0), -step.get("v", 0))
            found.append(got_ref[pl.ds(row + owner * 64, 1), :])
        row_ref[section : section + 1, :] = functools.reduce(jnp.maximum, found)
    columns = row_ref[...].T
    best = jnp.full((1, rows), NONE, jnp.float32)
    for section in range(SECTIONS):
        place = lax.broadcasted_iota(jnp.int32, (BOUND, rows), 0) + section * BOUND
        found = jnp.where(slot_ref[...] == place, columns[:BOUND, section : section + 1], NONE)
        best = jnp.maximum(best, jnp.max(found, 0, keepdims=True))
    out_ref[...] = best


def unsort(got, slot):
    vmem = pl.BlockSpec(memory_space=pltpu.VMEM)
    return pl.pallas_call(
        unsort_kernel,
        in_specs=[vmem] * 2,
        out_specs=vmem,
        out_shape=jax.ShapeDtypeStruct(slot.shape, jnp.float32),
        scratch_shapes=[pltpu.VMEM((LANES, LANES), jnp.float32)],
        name="unsort",
    )(got, slot)


def on_device(embeddings, cluster):
    mine, other, slot = sort_rows(embeddings, cluster.reshape(1, -1))

    def section(block, step):
        return block[step * BOUND : (step + 1) * BOUND]

    held = {}
    near = {step: take(section(mine, step), ring=-step) for step in (2, 1, 3)}
    far = {step: take(section(other, step), core=1, ring=-step) for step in (2, 1, 3, 0)}
    near[0] = section(mine, 0)
    held["0", "m"] = jnp.concatenate([near[step] for step in range(SIDE)], 0)
    held["0", "s"] = jnp.concatenate([far[step] for step in range(SIDE)], 0)
    sources = {
        "v1m": ("0m", {"v": 1}),
        "v1s": ("0s", {"v": 1}),
        "u1m": ("0m", {"u": 1}),
        "u1s": ("0s", {"u": 1}),
        "u3m": ("0m", {"u": -1}),
        "u3s": ("0s", {"u": -1}),
        "v2m": ("v1m", {"v": 1}),
        "v2s": ("v1s", {"v": 1}),
        "u2m": ("u3m", {"u": -1}) if CROSS else ("u1m", {"u": 1}),
        "u2s": ("u1s", {"u": 1}) if CROSS else ("u3s", {"u": -1}),
    }
    gated = {}

    def get(name):
        key = (name[:-1], name[-1])
        if key not in held:
            source, step = sources[name]
            held[key] = take(gated[name] if name in gated else get(source), **step)
        return held[key]

    def free(name):
        if name in sum((names for source, names in RELAYS.values()), ()):
            return name in gated
        return name[0] == "0" or free(sources[name][0])

    def fill():
        for name in ORDER:
            if free(name):
                get(name)

    fill()
    best = jnp.full((len(BLOCKS), SLOTS), NONE, jnp.float32)
    kinds = {
        "A": [("0", "ms", "0", "lane")],
        "B": [("u1", "ms", "0", "both")],
        "c": [("v1", "m", "0", "both")],
        "k": [("v1", "s", "0", "both")],
        "b": [("u1", "m", "0", "both")],
        "q": [("u1", "s", "0", "both")],
        "C": [("0", "ms", "v1", "both")],
        "D": [("u1", "ms", "v1", "both"), ("u3", "ms", "v1", "both")],
        "d": [("u1", "ms", "v1", "both")],
        "e": [("u3", "ms", "v1", "both")],
        "F": [("u2", "ms", "0", "lane"), ("u2", "ms", "v1", "both")],
        "G": [("v2", "m", near, "both") for near in ("0", "u1")],
        "g": [("v2", "m", "u2", "both")],
        "E": [("v2", "m", near, "both") for near in ("0", "u1", "u2")],
        "H": [("v2", "s", near, "both") for near in ("0", "u1", "u2")],
    }
    for k, letter in enumerate(PLAN):
        extra = [get(name) for name in DEPS.get(letter, ())]
        relay, names = RELAYS.get(letter, (None, ()))
        relay = (relay[:-1], relay[-1]) if relay else None
        best = pair_max(held, best, kinds[letter], k + 1 == len(PLAN), EFFORTS[k], extra, relay)
        if relay:
            best, copy = best
            gated.update({name: copy for name in names})
        fill()
    got = lax.all_to_all(best, AXES, 0, 0, tiled=True)
    return unsort(got, slot).reshape(-1)


def solution(mesh):
    in_specs = (P(AXES, None), P(AXES))
    return jax.shard_map(
        on_device, mesh=mesh, in_specs=in_specs, out_specs=P(AXES), check_vma=False
    )
```

```python
import functools

import jax
import jax.numpy as jnp
from jax import lax
from jax.experimental import pallas as pl
from jax.experimental.pallas import tpu as pltpu
from jax.sharding import PartitionSpec as P

AXES = ("group", "member")
SIDE = 4
CORES = 2
DEVICES = CORES * SIDE**3
BOUND = 96
HALF = SIDE * BOUND
SLOTS = CORES * HALF
TILE = 256
START = {"w": 0, "m": 0, "s": HALF}
STEPS = {
    "0": {"u": 0, "v": 0},
    "u1": {"u": 1},
    "u3": {"u": -1},
    "v1": {"v": 1},
    "u2": {"u": 2},
    "v2": {"v": 2},
}
BLOCKS = tuple(STEPS)
SECTIONS = 2 * SIDE
LANES = 128
CHUNKS = 4
ORDER = ('v1m', 'u1m', 'u3m', 'v1s', 'u1s', 'u3s', 'v2m', 'v2s', 'u2m', 'u2s')
CROSS = True
PLAN = 'AcbKDGxyH'
EFFORTS = (6, 6, 6, 6, 6, 6, 6, 6, 6)
DEPS = {'b': ('u3m',)}
RELAYS = {}
SORT_VMEM = 20
LOW = -8.0
NONE = -2.0


def place(device):
    return (device // 64, device // 16 % 4, device // 4 % 4, device % 4)


def device_at(core, z, y, x):
    return core * 64 + z % 4 * 16 + y % 4 * 4 + x % 4


def moved(device, core=0, ring=0, u=0, v=0):
    c, z, y, x = place(device)
    if c == 0:
        z, x, y = z + ring, x + u, y + v
    else:
        x, z, y = x + ring, z + u, y - v
    return device_at((c + core) % 2, z, y, x)


def take(block, **step):
    route = [(moved(device, **step), device) for device in range(DEVICES)]
    return lax.ppermute(block, AXES, route)


def here():
    member = lax.axis_index("member")
    return lax.axis_index("group"), member // 16, member // 4 % 4, member % 4


def partner(core, z, y, x, ring, u, v):
    ring = (jnp.where(core == 0, z, x) + ring) & 3
    u = (jnp.where(core == 0, x, z) + u) & 3
    y = (jnp.where(core == 0, y + v, y - v)) & 3
    return ring * jnp.where(core == 0, 16, 1) + u * jnp.where(core == 0, 1, 16) + y * 4


def sort_kernel(rows_hbm, cluster_hbm, mine_ref, other_ref, slot_ref, *scratch):
    rows_ref, cluster_ref, normed_ref, sems = scratch
    rows = rows_ref.shape[0]
    step = rows // CHUNKS
    copies = [pltpu.make_async_copy(cluster_hbm, cluster_ref, sems.at[CHUNKS])]
    for k in range(CHUNKS):
        part = pl.ds(k * step, step)
        copies.append(
            pltpu.make_async_copy(rows_hbm.at[part, :], rows_ref.at[part, :], sems.at[k])
        )
    for copy in copies:
        copy.start()
    core, z, y, x = here()
    ring_mine, ring_other = jnp.where(core == 0, z, x), jnp.where(core == 0, x, z)
    before = lax.broadcasted_iota(jnp.int32, (rows, rows), 0) < lax.broadcasted_iota(
        jnp.int32, (rows, rows), 1
    )
    before = jnp.where(before, 1.0, 0.0).astype(jnp.bfloat16)
    copies[0].wait()
    cluster = cluster_ref[...]
    hits = cluster == lax.broadcasted_iota(jnp.int32, (8, rows), 0)
    hits = jnp.where(hits, 1.0, 0.0)
    counted = jnp.dot(hits.astype(jnp.bfloat16), before, preferred_element_type=jnp.float32)
    rank = jnp.sum(counted * hits, 0, keepdims=True).astype(jnp.int32)
    is_mine = cluster // 4 == core
    turn = (cluster + 4 - jnp.where(is_mine, ring_mine, ring_other)) % 4
    slot = (jnp.where(is_mine, 0, 4) + turn) * BOUND + rank
    slot_ref[...] = slot
    for k in range(CHUNKS):
        copies[1 + k].wait()
        part = slice(k * step, (k + 1) * step)
        values = rows_ref[part, :].astype(jnp.float32)
        total = jnp.sum(values * values, 1, keepdims=True)
        normed_ref[part, :] = (values * lax.rsqrt(total + 1e-06)).astype(jnp.bfloat16)
    normed = normed_ref[...]
    for start, out_ref in ((0, mine_ref), (HALF, other_ref)):
        picks = slot - start == lax.broadcasted_iota(jnp.int32, (HALF, rows), 0)
        picks = jnp.where(picks, 1.0, 0.0)
        used = jnp.max(picks, 1, keepdims=True)
        placed = jnp.dot(picks.astype(jnp.bfloat16), normed, preferred_element_type=jnp.float32)
        first = lax.broadcasted_iota(jnp.int32, (HALF, LANES), 1) == 0
        head = jnp.where(first & (used < 0.5), 2.0, placed[:, :LANES])
        out_ref[:, :LANES] = head.astype(jnp.bfloat16)
        out_ref[:, LANES:] = placed[:, LANES:].astype(jnp.bfloat16)


def sort_rows(embeddings, cluster):
    rows, width = embeddings.shape
    vmem = pl.BlockSpec(memory_space=pltpu.VMEM)
    hbm = pl.BlockSpec(memory_space=pltpu.HBM)
    return pl.pallas_call(
        sort_kernel,
        in_specs=[hbm, hbm],
        out_specs=[vmem] * 3,
        out_shape=[
            jax.ShapeDtypeStruct((HALF, width), jnp.bfloat16),
            jax.ShapeDtypeStruct((HALF, width), jnp.bfloat16),
            jax.ShapeDtypeStruct((1, rows), jnp.int32),
        ],
        scratch_shapes=[
            pltpu.VMEM((rows, width), jnp.bfloat16),
            pltpu.VMEM((1, rows), jnp.int32),
            pltpu.VMEM((rows, width), jnp.bfloat16),
            pltpu.SemaphoreType.DMA((CHUNKS + 1,)),
        ],
        compiler_params=pltpu.CompilerParams(vmem_limit_bytes=SORT_VMEM << 20),
        cost_estimate=pl.CostEstimate(
            flops=4 * rows * HALF * width, bytes_accessed=6 * rows * width, transcendentals=rows
        ),
        name="sort_rows",
    )(embeddings, cluster)


def empty(values):
    return jnp.where(values[:, :LANES].astype(jnp.float32) > 1.5, LOW, 0.0)


def pair_kernel(names, blocks, products, relay, *refs):
    chunks = dict(zip(names, refs))
    before_ref = refs[len(names)]
    best_ref, fold_ref, lane_ref = refs[-3:]
    if relay:
        best_ref, copy_ref = refs[-4:-2]
        copy_ref[...] = chunks[relay][...]
    fold_blocks = {upper for upper, parts, lower, kind in products if kind != "lane"}
    lane_blocks = {lower for upper, parts, lower, kind in products if kind != "fold"}
    for block in fold_blocks:
        fold_ref[blocks.index(block)] = jnp.full(fold_ref.shape[1:], LOW, jnp.float32)
    for block in lane_blocks:
        lane_ref[blocks.index(block)] = jnp.full(lane_ref.shape[1:], LOW, jnp.float32)
    for upper, parts, lower, kind in products:
        for tile in range(SLOTS // TILE):
            columns = slice(tile * TILE, (tile + 1) * TILE)
            if (lower, "w") in chunks:
                right = chunks[lower, "w"][columns, :]
            elif tile == 0:
                right = chunks[lower, "m"][:TILE, :]
            elif tile == 1:
                first, second = chunks[lower, "m"], chunks[lower, "s"]
                right = jnp.concatenate([first[TILE:, :], second[: TILE // 2, :]], 0)
            else:
                right = chunks[lower, "s"][TILE // 2 :, :]
            if kind != "lane":
                across = empty(right).T[:1, :]
            for part in parts:
                values = chunks[upper, part][...]
                rows = values.shape[0]
                scores = lax.dot_general(
                    values, right, (((1,), (1,)), ((), ())), preferred_element_type=jnp.float32
                )
                if upper == lower:
                    row = lax.broadcasted_iota(jnp.int32, scores.shape, 0) + START[part]
                    column = lax.broadcasted_iota(jnp.int32, scores.shape, 1) + tile * TILE
                    scores = jnp.where(row == column, LOW, scores)
                if kind != "fold":
                    at = blocks.index(lower)
                    down = scores + empty(values)[:, :1]
                    down = jnp.max(down.reshape(rows // 8, 8, TILE), 0)
                    lane_ref[at, :, columns] = jnp.maximum(lane_ref[at, :, columns], down)
                if kind != "lane":
                    at = (blocks.index(upper), slice(START[part], START[part] + rows))
                    over = scores + across
                    over = jnp.maximum(over[:, :LANES], over[:, LANES:])
                    fold_ref[at] = jnp.maximum(fold_ref[at], over)
    best = [before_ref[k : k + 1, :] for k in range(len(BLOCKS))]
    for block in blocks:
        at, k = blocks.index(block), BLOCKS.index(block)
        if block in fold_blocks:
            best[k] = jnp.maximum(best[k], jnp.max(fold_ref[at].T, 0, keepdims=True))
        if block in lane_blocks:
            best[k] = jnp.maximum(best[k], jnp.max(lane_ref[at], 0, keepdims=True))
    if best_ref.shape[0] == len(BLOCKS):
        best_ref[...] = jnp.concatenate(best, 0)
        return
    best_ref[...] = jnp.full(best_ref.shape, NONE, jnp.float32)
    core, z, y, x = here()
    for section in range(SECTIONS):
        half, turn = section // SIDE, section % SIDE
        for k, step in enumerate(STEPS.values()):
            row = partner(core, z, y, x, -turn, step.get("u", 0), step.get("v", 0))
            row += (core if half == 0 else 1 - core) * 64
            best_ref[pl.ds(row, 1), :BOUND] = best[k][:, section * BOUND : (section + 1) * BOUND]


def pair_max(held, before, products, last, effort, extra, relay):
    names, blocks = [relay] * bool(relay), []
    for upper, parts, lower, kind in products:
        names += [(upper, part) for part in parts]
        names += [(lower, part) for part in "wms" if (lower, part) in held]
        blocks += [lower] * (kind != "fold") + [upper] * (kind != "lane")
    names, blocks = list(dict.fromkeys(names)), list(dict.fromkeys(blocks))
    vmem = pl.BlockSpec(memory_space=pltpu.VMEM)
    width = held[names[0]].shape[1]
    pairs = sum(
        held[upper, part].shape[0] * SLOTS
        for upper, parts, lower, kind in products
        for part in parts
    )
    shape = (DEVICES, LANES) if last else before.shape
    return pl.pallas_call(
        functools.partial(pair_kernel, names, blocks, products, relay),
        in_specs=[vmem] * (len(names) + 1)
        + [pl.BlockSpec(memory_space=pl.ANY)] * len(extra),
        out_specs=[vmem, vmem] if relay else vmem,
        out_shape=[
            jax.ShapeDtypeStruct(shape, jnp.float32),
            jax.ShapeDtypeStruct((HALF, width), jnp.bfloat16),
        ]
        if relay
        else jax.ShapeDtypeStruct(shape, jnp.float32),
        scratch_shapes=[
            pltpu.VMEM((len(blocks), SLOTS, LANES), jnp.float32),
            pltpu.VMEM((len(blocks), 8, SLOTS), jnp.float32),
        ],
        compiler_params=pltpu.CompilerParams(vmem_limit_bytes=20 << 20),
        cost_estimate=pl.CostEstimate(
            flops=int(2 * effort * pairs * width),
            bytes_accessed=2 * len(names) * HALF * width,
            transcendentals=0,
        ),
        name="pair_max",
    )(*(held[name] for name in names), before, *extra)


def unsort_kernel(got_ref, slot_ref, out_ref, row_ref):
    rows = slot_ref.shape[1]
    core, z, y, x = here()
    row_ref[...] = jnp.full(row_ref.shape, NONE, jnp.float32)
    for section in range(SECTIONS):
        half, turn = section // SIDE, section % SIDE
        owner = core if half == 0 else 1 - core
        found = []
        for step in STEPS.values():
            row = partner(owner, z, y, x, turn, -step.get("u", 0), -step.get("v", 0))
            found.append(got_ref[pl.ds(row + owner * 64, 1), :])
        row_ref[section : section + 1, :] = functools.reduce(jnp.maximum, found)
    columns = row_ref[...].T
    best = jnp.full((1, rows), NONE, jnp.float32)
    for section in range(SECTIONS):
        place = lax.broadcasted_iota(jnp.int32, (BOUND, rows), 0) + section * BOUND
        found = jnp.where(slot_ref[...] == place, columns[:BOUND, section : section + 1], NONE)
        best = jnp.maximum(best, jnp.max(found, 0, keepdims=True))
    out_ref[...] = best


def unsort(got, slot):
    vmem = pl.BlockSpec(memory_space=pltpu.VMEM)
    return pl.pallas_call(
        unsort_kernel,
        in_specs=[vmem] * 2,
        out_specs=vmem,
        out_shape=jax.ShapeDtypeStruct(slot.shape, jnp.float32),
        scratch_shapes=[pltpu.VMEM((LANES, LANES), jnp.float32)],
        name="unsort",
    )(got, slot)


def on_device(embeddings, cluster):
    mine, other, slot = sort_rows(embeddings, cluster.reshape(1, -1))

    def section(block, step):
        return block[step * BOUND : (step + 1) * BOUND]

    held = {}
    near = {step: take(section(mine, step), ring=-step) for step in (2, 1, 3)}
    far = {step: take(section(other, step), core=1, ring=-step) for step in (2, 1, 3, 0)}
    near[0] = section(mine, 0)
    held["0", "m"] = jnp.concatenate([near[step] for step in range(SIDE)], 0)
    held["0", "s"] = jnp.concatenate([far[step] for step in range(SIDE)], 0)
    sources = {
        "v1m": ("0m", {"v": 1}),
        "v1s": ("0s", {"v": 1}),
        "u1m": ("0m", {"u": 1}),
        "u1s": ("0s", {"u": 1}),
        "u3m": ("0m", {"u": -1}),
        "u3s": ("0s", {"u": -1}),
        "v2m": ("v1m", {"v": 1}),
        "v2s": ("v1s", {"v": 1}),
        "u2m": ("u3m", {"u": -1}) if CROSS else ("u1m", {"u": 1}),
        "u2s": ("u1s", {"u": 1}) if CROSS else ("u3s", {"u": -1}),
    }
    gated = {}

    def get(name):
        key = (name[:-1], name[-1])
        if key not in held:
            source, step = sources[name]
            held[key] = take(gated[name] if name in gated else get(source), **step)
        return held[key]

    def free(name):
        if name in sum((names for source, names in RELAYS.values()), ()):
            return name in gated
        return name[0] == "0" or free(sources[name][0])

    def fill():
        for name in ORDER:
            if free(name):
                get(name)

    fill()
    best = jnp.full((len(BLOCKS), SLOTS), NONE, jnp.float32)
    kinds = {
        "A": [("0", "ms", "0", "lane")],
        "B": [("u1", "ms", "0", "both")],
        "c": [("v1", "m", "0", "both")],
        "k": [("v1", "s", "0", "both")],
        "b": [("u1", "m", "0", "both")],
        "q": [("u1", "s", "0", "both")],
        "C": [("0", "ms", "v1", "both")],
        "D": [("u1", "ms", "v1", "both"), ("u3", "ms", "v1", "both")],
        "d": [("u1", "ms", "v1", "both")],
        "e": [("u3", "ms", "v1", "both")],
        "F": [("u2", "ms", "0", "lane"), ("u2", "ms", "v1", "both")],
        "G": [("v2", "m", near, "both") for near in ("0", "u1")],
        "g": [("v2", "m", "u2", "both")],
        "f": [("u2", "ms", "0", "lane"), ("u2", "ms", "v1", "both"), ("v2", "m", "u2", "both")],
        "K": [("v1", "s", "0", "both"), ("u1", "s", "0", "both")],
        "W": [("v1", "m", "0", "both"), ("u1", "m", "0", "both")],
        "x": [("u2", "m", "0", "lane"), ("u2", "m", "v1", "both")],
        "y": [("u2", "s", "0", "lane"), ("u2", "s", "v1", "both"), ("v2", "m", "u2", "both")],
        "E": [("v2", "m", near, "both") for near in ("0", "u1", "u2")],
        "H": [("v2", "s", near, "both") for near in ("0", "u1", "u2")],
    }
    for k, letter in enumerate(PLAN):
        extra = [get(name) for name in DEPS.get(letter, ())]
        relay, names = RELAYS.get(letter, (None, ()))
        relay = (relay[:-1], relay[-1]) if relay else None
        best = pair_max(held, best, kinds[letter], k + 1 == len(PLAN), EFFORTS[k], extra, relay)
        if relay:
            best, copy = best
            gated.update({name: copy for name in names})
        fill()
    got = lax.all_to_all(best, AXES, 0, 0, tiled=True)
    return unsort(got, slot).reshape(-1)


def solution(mesh):
    in_specs = (P(AXES, None), P(AXES))
    return jax.shard_map(
        on_device, mesh=mesh, in_specs=in_specs, out_specs=P(AXES), check_vma=False
    )
```

```python
import functools

import jax
import jax.numpy as jnp
from jax import lax
from jax.experimental import pallas as pl
from jax.experimental.pallas import tpu as pltpu
from jax.sharding import PartitionSpec as P

AXES = ("group", "member")
SIDE = 4
CORES = 2
DEVICES = CORES * SIDE**3
BOUND = 96
HALF = SIDE * BOUND
SLOTS = CORES * HALF
TILE = 256
START = {"w": 0, "m": 0, "s": HALF}
STEPS = {
    "0": {"u": 0, "v": 0},
    "u1": {"u": 1},
    "u3": {"u": -1},
    "v1": {"v": 1},
    "u2": {"u": 2},
    "v2": {"v": 2},
}
BLOCKS = tuple(STEPS)
SECTIONS = 2 * SIDE
LANES = 128
CHUNKS = 4
EFFORT = 6
LOW = -8.0
NONE = -2.0


def place(device):
    return (device // 64, device // 16 % 4, device // 4 % 4, device % 4)


def device_at(core, z, y, x):
    return core * 64 + z % 4 * 16 + y % 4 * 4 + x % 4


def moved(device, core=0, ring=0, u=0, v=0):
    c, z, y, x = place(device)
    if c == 0:
        z, x, y = z + ring, x + u, y + v
    else:
        x, z, y = x + ring, z + u, y - v
    return device_at((c + core) % 2, z, y, x)


def take(block, **step):
    route = [(moved(device, **step), device) for device in range(DEVICES)]
    return lax.ppermute(block, AXES, route)


def here():
    member = lax.axis_index("member")
    return lax.axis_index("group"), member // 16, member // 4 % 4, member % 4


def partner(core, z, y, x, ring, u, v):
    ring = (jnp.where(core == 0, z, x) + ring) & 3
    u = (jnp.where(core == 0, x, z) + u) & 3
    y = (jnp.where(core == 0, y + v, y - v)) & 3
    return ring * jnp.where(core == 0, 16, 1) + u * jnp.where(core == 0, 1, 16) + y * 4


def sort_kernel(rows_hbm, cluster_hbm, mine_ref, other_ref, slot_ref, *scratch):
    rows_ref, cluster_ref, normed_ref, sems = scratch
    rows = rows_ref.shape[0]
    step = rows // CHUNKS
    copies = [pltpu.make_async_copy(cluster_hbm, cluster_ref, sems.at[CHUNKS])]
    for k in range(CHUNKS):
        part = pl.ds(k * step, step)
        copies.append(
            pltpu.make_async_copy(rows_hbm.at[part, :], rows_ref.at[part, :], sems.at[k])
        )
    for copy in copies:
        copy.start()
    core, z, y, x = here()
    ring_mine, ring_other = jnp.where(core == 0, z, x), jnp.where(core == 0, x, z)
    before = lax.broadcasted_iota(jnp.int32, (rows, rows), 0) < lax.broadcasted_iota(
        jnp.int32, (rows, rows), 1
    )
    before = jnp.where(before, 1.0, 0.0).astype(jnp.bfloat16)
    copies[0].wait()
    cluster = cluster_ref[...]
    hits = cluster == lax.broadcasted_iota(jnp.int32, (8, rows), 0)
    hits = jnp.where(hits, 1.0, 0.0)
    counted = jnp.dot(hits.astype(jnp.bfloat16), before, preferred_element_type=jnp.float32)
    rank = jnp.sum(counted * hits, 0, keepdims=True).astype(jnp.int32)
    is_mine = cluster // 4 == core
    turn = (cluster + 4 - jnp.where(is_mine, ring_mine, ring_other)) % 4
    slot = (jnp.where(is_mine, 0, 4) + turn) * BOUND + rank
    slot_ref[...] = slot
    for k in range(CHUNKS):
        copies[1 + k].wait()
        part = slice(k * step, (k + 1) * step)
        values = rows_ref[part, :].astype(jnp.float32)
        total = jnp.sum(values * values, 1, keepdims=True)
        normed_ref[part, :] = (values * lax.rsqrt(total + 1e-06)).astype(jnp.bfloat16)
    normed = normed_ref[...]
    for start, out_ref in ((0, mine_ref), (HALF, other_ref)):
        picks = slot - start == lax.broadcasted_iota(jnp.int32, (HALF, rows), 0)
        picks = jnp.where(picks, 1.0, 0.0)
        used = jnp.max(picks, 1, keepdims=True)
        placed = jnp.dot(picks.astype(jnp.bfloat16), normed, preferred_element_type=jnp.float32)
        first = lax.broadcasted_iota(jnp.int32, (HALF, LANES), 1) == 0
        head = jnp.where(first & (used < 0.5), 2.0, placed[:, :LANES])
        out_ref[:, :LANES] = head.astype(jnp.bfloat16)
        out_ref[:, LANES:] = placed[:, LANES:].astype(jnp.bfloat16)


def sort_rows(embeddings, cluster):
    rows, width = embeddings.shape
    vmem = pl.BlockSpec(memory_space=pltpu.VMEM)
    hbm = pl.BlockSpec(memory_space=pltpu.HBM)
    return pl.pallas_call(
        sort_kernel,
        in_specs=[hbm, hbm],
        out_specs=[vmem] * 3,
        out_shape=[
            jax.ShapeDtypeStruct((HALF, width), jnp.bfloat16),
            jax.ShapeDtypeStruct((HALF, width), jnp.bfloat16),
            jax.ShapeDtypeStruct((1, rows), jnp.int32),
        ],
        scratch_shapes=[
            pltpu.VMEM((rows, width), jnp.bfloat16),
            pltpu.VMEM((1, rows), jnp.int32),
            pltpu.VMEM((rows, width), jnp.bfloat16),
            pltpu.SemaphoreType.DMA((CHUNKS + 1,)),
        ],
        compiler_params=pltpu.CompilerParams(vmem_limit_bytes=20 << 20),
        cost_estimate=pl.CostEstimate(
            flops=4 * rows * HALF * width, bytes_accessed=6 * rows * width, transcendentals=rows
        ),
        name="sort_rows",
    )(embeddings, cluster)


def empty(values):
    return jnp.where(values[:, :LANES].astype(jnp.float32) > 1.5, LOW, 0.0)


def pair_kernel(names, blocks, products, *refs):
    chunks = dict(zip(names, refs))
    before_ref = refs[len(names)]
    best_ref, fold_ref, lane_ref = refs[-3:]
    fold_blocks = {upper for upper, parts, lower, kind, *tiles in products if kind != "lane"}
    lane_blocks = {lower for upper, parts, lower, kind, *tiles in products if kind != "fold"}
    for block in fold_blocks:
        fold_ref[blocks.index(block)] = jnp.full(fold_ref.shape[1:], LOW, jnp.float32)
    for block in lane_blocks:
        lane_ref[blocks.index(block)] = jnp.full(lane_ref.shape[1:], LOW, jnp.float32)
    for upper, parts, lower, kind, *tiles in products:
        for tile in tiles or range(SLOTS // TILE):
            columns = slice(tile * TILE, (tile + 1) * TILE)
            if tile == 0:
                right = chunks[lower, "m"][:TILE, :]
            elif tile == 1:
                first, second = chunks[lower, "m"], chunks[lower, "s"]
                right = jnp.concatenate([first[TILE:, :], second[: TILE // 2, :]], 0)
            else:
                right = chunks[lower, "s"][TILE // 2 :, :]
            if kind != "lane":
                across = empty(right).T[:1, :]
            for part in parts:
                values = chunks[upper, part][...]
                rows = values.shape[0]
                scores = lax.dot_general(
                    values, right, (((1,), (1,)), ((), ())), preferred_element_type=jnp.float32
                )
                if upper == lower:
                    row = lax.broadcasted_iota(jnp.int32, scores.shape, 0) + START[part]
                    column = lax.broadcasted_iota(jnp.int32, scores.shape, 1) + tile * TILE
                    scores = jnp.where(row == column, LOW, scores)
                if kind != "fold":
                    at = blocks.index(lower)
                    down = scores + empty(values)[:, :1]
                    down = jnp.max(down.reshape(rows // 8, 8, TILE), 0)
                    lane_ref[at, :, columns] = jnp.maximum(lane_ref[at, :, columns], down)
                if kind != "lane":
                    at = (blocks.index(upper), slice(START[part], START[part] + rows))
                    over = scores + across
                    over = jnp.maximum(over[:, :LANES], over[:, LANES:])
                    fold_ref[at] = jnp.maximum(fold_ref[at], over)
    best = [before_ref[k : k + 1, :] for k in range(len(BLOCKS))]
    for block in blocks:
        at, k = blocks.index(block), BLOCKS.index(block)
        if block in fold_blocks:
            best[k] = jnp.maximum(best[k], jnp.max(fold_ref[at].T, 0, keepdims=True))
        if block in lane_blocks:
            best[k] = jnp.maximum(best[k], jnp.max(lane_ref[at], 0, keepdims=True))
    if best_ref.shape[0] == len(BLOCKS):
        best_ref[...] = jnp.concatenate(best, 0)
        return
    best_ref[...] = jnp.full(best_ref.shape, NONE, jnp.float32)
    core, z, y, x = here()
    for section in range(SECTIONS):
        half, turn = section // SIDE, section % SIDE
        for k, step in enumerate(STEPS.values()):
            row = partner(core, z, y, x, -turn, step.get("u", 0), step.get("v", 0))
            row += (core if half == 0 else 1 - core) * 64
            best_ref[pl.ds(row, 1), :BOUND] = best[k][:, section * BOUND : (section + 1) * BOUND]


def pair_max(held, before, products, last, extra):
    names, blocks = [], []
    for upper, parts, lower, kind, *tiles in products:
        names += [(upper, part) for part in parts]
        names += [(lower, "m"), (lower, "s")]
        blocks += [lower] * (kind != "fold") + [upper] * (kind != "lane")
    names, blocks = list(dict.fromkeys(names)), list(dict.fromkeys(blocks))
    vmem = pl.BlockSpec(memory_space=pltpu.VMEM)
    width = held[names[0]].shape[1]
    pairs = sum(
        held[upper, part].shape[0] * (TILE * len(tiles) if tiles else SLOTS)
        for upper, parts, lower, kind, *tiles in products
        for part in parts
    )
    shape = (DEVICES, LANES) if last else before.shape
    return pl.pallas_call(
        functools.partial(pair_kernel, names, blocks, products),
        in_specs=[vmem] * (len(names) + 1)
        + [pl.BlockSpec(memory_space=pl.ANY)] * len(extra),
        out_specs=vmem,
        out_shape=jax.ShapeDtypeStruct(shape, jnp.float32),
        scratch_shapes=[
            pltpu.VMEM((len(blocks), SLOTS, LANES), jnp.float32),
            pltpu.VMEM((len(blocks), 8, SLOTS), jnp.float32),
        ],
        compiler_params=pltpu.CompilerParams(vmem_limit_bytes=20 << 20),
        cost_estimate=pl.CostEstimate(
            flops=2 * EFFORT * pairs * width,
            bytes_accessed=2 * len(names) * HALF * width,
            transcendentals=0,
        ),
        name="pair_max",
    )(*(held[name] for name in names), before, *extra)


def unsort_kernel(got_ref, slot_ref, out_ref, row_ref):
    rows = slot_ref.shape[1]
    core, z, y, x = here()
    row_ref[...] = jnp.full(row_ref.shape, NONE, jnp.float32)
    for section in range(SECTIONS):
        half, turn = section // SIDE, section % SIDE
        owner = core if half == 0 else 1 - core
        found = []
        for step in STEPS.values():
            row = partner(owner, z, y, x, turn, -step.get("u", 0), -step.get("v", 0))
            found.append(got_ref[pl.ds(row + owner * 64, 1), :])
        row_ref[section : section + 1, :] = functools.reduce(jnp.maximum, found)
    columns = row_ref[...].T
    best = jnp.full((1, rows), NONE, jnp.float32)
    for section in range(SECTIONS):
        place = lax.broadcasted_iota(jnp.int32, (BOUND, rows), 0) + section * BOUND
        found = jnp.where(slot_ref[...] == place, columns[:BOUND, section : section + 1], NONE)
        best = jnp.maximum(best, jnp.max(found, 0, keepdims=True))
    out_ref[...] = best


def unsort(got, slot):
    vmem = pl.BlockSpec(memory_space=pltpu.VMEM)
    return pl.pallas_call(
        unsort_kernel,
        in_specs=[vmem] * 2,
        out_specs=vmem,
        out_shape=jax.ShapeDtypeStruct(slot.shape, jnp.float32),
        scratch_shapes=[pltpu.VMEM((LANES, LANES), jnp.float32)],
        name="unsort",
    )(got, slot)


def on_device(embeddings, cluster):
    mine, other, slot = sort_rows(embeddings, cluster.reshape(1, -1))

    def section(block, step):
        return block[step * BOUND : (step + 1) * BOUND]

    held = {}
    near = {step: take(section(mine, step), ring=-step) for step in (2, 1, 3)}
    far = {step: take(section(other, step), core=1, ring=-step) for step in (2, 1, 3, 0)}
    near[0] = section(mine, 0)
    held["0", "m"] = jnp.concatenate([near[step] for step in range(SIDE)], 0)
    held["0", "s"] = jnp.concatenate([far[step] for step in range(SIDE)], 0)
    for part in "ms":
        held["v1", part] = take(held["0", part], v=1)
        held["u1", part] = take(held["0", part], u=1)
        held["u3", part] = take(held["0", part], u=-1)
    held["v2", "m"] = take(held["v1", "m"], v=1)
    held["v2", "s"] = take(held["v1", "s"], v=1)
    held["u2", "m"] = take(held["u3", "m"], u=-1)
    held["u2", "s"] = take(held["u1", "s"], u=1)

    plan = (
        ([("0", "ms", "0", "lane")], []),
        ([("v1", "m", "0", "both")], []),
        ([("u1", "m", "0", "both")], [held["u3", "m"]]),
        ([("v1", "s", "0", "both"), ("u1", "s", "0", "both")], []),
        ([("u1", "ms", "v1", "both"), ("u3", "ms", "v1", "both")], []),
        ([("v2", "m", "0", "both", 0, 1), ("v2", "m", "u1", "both")], []),
        ([("u2", "m", "0", "lane", 0, 1), ("u2", "m", "v1", "both")], []),
        (
            [
                ("u2", "s", "0", "both"),
                ("u2", "s", "v1", "both"),
                ("v2", "m", "u2", "both", 0, 1),
            ],
            [],
        ),
        ([("v2", "s", near, "both") for near in ("0", "u1", "u2")], []),
    )
    best = jnp.full((len(BLOCKS), SLOTS), NONE, jnp.float32)
    for k, (products, extra) in enumerate(plan):
        best = pair_max(held, best, products, k + 1 == len(plan), extra)
    got = lax.all_to_all(best, AXES, 0, 0, tiled=True)
    return unsort(got, slot).reshape(-1)


def solution(mesh):
    in_specs = (P(AXES, None), P(AXES))
    return jax.shard_map(
        on_device, mesh=mesh, in_specs=in_specs, out_specs=P(AXES), check_vma=False
    )
```

```python
import functools

import jax
import jax.numpy as jnp
from jax import lax
from jax.experimental import pallas as pl
from jax.experimental.pallas import tpu as pltpu
from jax.sharding import PartitionSpec as P

AXES = ("group", "member")
SIDE = 4
CORES = 2
DEVICES = CORES * SIDE**3
BOUND = 96
HALF = SIDE * BOUND
SLOTS = CORES * HALF
TILE = 256
START = {"w": 0, "m": 0, "s": HALF}
STEPS = {
    "0": {"u": 0, "v": 0},
    "u1": {"u": 1},
    "u3": {"u": -1},
    "v1": {"v": 1},
    "u2": {"u": 2},
    "v2": {"v": 2},
}
BLOCKS = tuple(STEPS)
SECTIONS = 2 * SIDE
LANES = 128
EFFORT = 6
LOW = -8.0
NONE = -2.0


def place(device):
    return (device // 64, device // 16 % 4, device // 4 % 4, device % 4)


def device_at(core, z, y, x):
    return core * 64 + z % 4 * 16 + y % 4 * 4 + x % 4


def moved(device, core=0, ring=0, u=0, v=0):
    c, z, y, x = place(device)
    if c == 0:
        z, x, y = z + ring, x + u, y + v
    else:
        x, z, y = x + ring, z + u, y - v
    return device_at((c + core) % 2, z, y, x)


def take(block, **step):
    route = [(moved(device, **step), device) for device in range(DEVICES)]
    return lax.ppermute(block, AXES, route)


def here():
    member = lax.axis_index("member")
    return lax.axis_index("group"), member // 16, member // 4 % 4, member % 4


def partner(core, z, y, x, ring, u, v):
    ring = (jnp.where(core == 0, z, x) + ring) & 3
    u = (jnp.where(core == 0, x, z) + u) & 3
    y = (jnp.where(core == 0, y + v, y - v)) & 3
    return ring * jnp.where(core == 0, 16, 1) + u * jnp.where(core == 0, 1, 16) + y * 4


def sort_kernel(rows_ref, cluster_ref, mine_ref, other_ref, slot_ref):
    rows = rows_ref.shape[0]
    core, z, y, x = here()
    ring_mine, ring_other = jnp.where(core == 0, z, x), jnp.where(core == 0, x, z)
    before = lax.broadcasted_iota(jnp.int32, (rows, rows), 0) < lax.broadcasted_iota(
        jnp.int32, (rows, rows), 1
    )
    before = jnp.where(before, 1.0, 0.0).astype(jnp.bfloat16)
    cluster = cluster_ref[...]
    hits = cluster == lax.broadcasted_iota(jnp.int32, (8, rows), 0)
    hits = jnp.where(hits, 1.0, 0.0)
    counted = jnp.dot(hits.astype(jnp.bfloat16), before, preferred_element_type=jnp.float32)
    rank = jnp.sum(counted * hits, 0, keepdims=True).astype(jnp.int32)
    is_mine = cluster // 4 == core
    turn = (cluster + 4 - jnp.where(is_mine, ring_mine, ring_other)) % 4
    slot = (jnp.where(is_mine, 0, 4) + turn) * BOUND + rank
    slot_ref[...] = slot
    values = rows_ref[...].astype(jnp.float32)
    total = jnp.sum(values * values, 1, keepdims=True)
    normed = (values * lax.rsqrt(total + 1e-06)).astype(jnp.bfloat16)
    for start, out_ref in ((0, mine_ref), (HALF, other_ref)):
        picks = slot - start == lax.broadcasted_iota(jnp.int32, (HALF, rows), 0)
        picks = jnp.where(picks, 1.0, 0.0)
        used = jnp.max(picks, 1, keepdims=True)
        placed = jnp.dot(picks.astype(jnp.bfloat16), normed, preferred_element_type=jnp.float32)
        first = lax.broadcasted_iota(jnp.int32, (HALF, LANES), 1) == 0
        head = jnp.where(first & (used < 0.5), 2.0, placed[:, :LANES])
        out_ref[:, :LANES] = head.astype(jnp.bfloat16)
        out_ref[:, LANES:] = placed[:, LANES:].astype(jnp.bfloat16)


def sort_rows(embeddings, cluster):
    rows, width = embeddings.shape
    vmem = pl.BlockSpec(memory_space=pltpu.VMEM)
    return pl.pallas_call(
        sort_kernel,
        in_specs=[vmem, vmem],
        out_specs=[vmem] * 3,
        out_shape=[
            jax.ShapeDtypeStruct((HALF, width), jnp.bfloat16),
            jax.ShapeDtypeStruct((HALF, width), jnp.bfloat16),
            jax.ShapeDtypeStruct((1, rows), jnp.int32),
        ],
        compiler_params=pltpu.CompilerParams(vmem_limit_bytes=20 << 20),
        cost_estimate=pl.CostEstimate(
            flops=4 * rows * HALF * width, bytes_accessed=6 * rows * width, transcendentals=rows
        ),
        name="sort_rows",
    )(embeddings, cluster)


def empty(values):
    return jnp.where(values[:, :LANES].astype(jnp.float32) > 1.5, LOW, 0.0)


def pair_kernel(names, blocks, products, *refs):
    chunks = dict(zip(names, refs))
    before_ref = refs[len(names)]
    best_ref, fold_ref, lane_ref = refs[-3:]
    fold_blocks = {upper for upper, parts, lower, kind, *tiles in products if kind != "lane"}
    lane_blocks = {lower for upper, parts, lower, kind, *tiles in products if kind != "fold"}
    for block in fold_blocks:
        fold_ref[blocks.index(block)] = jnp.full(fold_ref.shape[1:], LOW, jnp.float32)
    for block in lane_blocks:
        lane_ref[blocks.index(block)] = jnp.full(lane_ref.shape[1:], LOW, jnp.float32)
    for upper, parts, lower, kind, *tiles in products:
        for tile in tiles or range(SLOTS // TILE):
            columns = slice(tile * TILE, (tile + 1) * TILE)
            if tile == 0:
                right = chunks[lower, "m"][:TILE, :]
            elif tile == 1:
                first, second = chunks[lower, "m"], chunks[lower, "s"]
                right = jnp.concatenate([first[TILE:, :], second[: TILE // 2, :]], 0)
            else:
                right = chunks[lower, "s"][TILE // 2 :, :]
            if kind != "lane":
                across = empty(right).T[:1, :]
            for part in parts:
                values = chunks[upper, part][...]
                rows = values.shape[0]
                scores = lax.dot_general(
                    values, right, (((1,), (1,)), ((), ())), preferred_element_type=jnp.float32
                )
                if upper == lower:
                    row = lax.broadcasted_iota(jnp.int32, scores.shape, 0) + START[part]
                    column = lax.broadcasted_iota(jnp.int32, scores.shape, 1) + tile * TILE
                    scores = jnp.where(row == column, LOW, scores)
                if kind != "fold":
                    at = blocks.index(lower)
                    down = scores + empty(values)[:, :1]
                    down = jnp.max(down.reshape(rows // 8, 8, TILE), 0)
                    lane_ref[at, :, columns] = jnp.maximum(lane_ref[at, :, columns], down)
                if kind != "lane":
                    at = (blocks.index(upper), slice(START[part], START[part] + rows))
                    over = scores + across
                    over = jnp.maximum(over[:, :LANES], over[:, LANES:])
                    fold_ref[at] = jnp.maximum(fold_ref[at], over)
    best = [before_ref[k : k + 1, :] for k in range(len(BLOCKS))]
    for block in blocks:
        at, k = blocks.index(block), BLOCKS.index(block)
        if block in fold_blocks:
            best[k] = jnp.maximum(best[k], jnp.max(fold_ref[at].T, 0, keepdims=True))
        if block in lane_blocks:
            best[k] = jnp.maximum(best[k], jnp.max(lane_ref[at], 0, keepdims=True))
    if best_ref.shape[0] == len(BLOCKS):
        best_ref[...] = jnp.concatenate(best, 0)
        return
    best_ref[...] = jnp.full(best_ref.shape, NONE, jnp.float32)
    core, z, y, x = here()
    for section in range(SECTIONS):
        half, turn = section // SIDE, section % SIDE
        for k, step in enumerate(STEPS.values()):
            row = partner(core, z, y, x, -turn, step.get("u", 0), step.get("v", 0))
            row += (core if half == 0 else 1 - core) * 64
            best_ref[pl.ds(row, 1), :BOUND] = best[k][:, section * BOUND : (section + 1) * BOUND]


def pair_max(held, before, products, last, extra):
    names, blocks = [], []
    for upper, parts, lower, kind, *tiles in products:
        names += [(upper, part) for part in parts]
        names += [(lower, "m"), (lower, "s")]
        blocks += [lower] * (kind != "fold") + [upper] * (kind != "lane")
    names, blocks = list(dict.fromkeys(names)), list(dict.fromkeys(blocks))
    vmem = pl.BlockSpec(memory_space=pltpu.VMEM)
    width = held[names[0]].shape[1]
    pairs = sum(
        held[upper, part].shape[0] * (TILE * len(tiles) if tiles else SLOTS)
        for upper, parts, lower, kind, *tiles in products
        for part in parts
    )
    shape = (DEVICES, LANES) if last else before.shape
    return pl.pallas_call(
        functools.partial(pair_kernel, names, blocks, products),
        in_specs=[vmem] * (len(names) + 1)
        + [pl.BlockSpec(memory_space=pl.ANY)] * len(extra),
        out_specs=vmem,
        out_shape=jax.ShapeDtypeStruct(shape, jnp.float32),
        scratch_shapes=[
            pltpu.VMEM((len(blocks), SLOTS, LANES), jnp.float32),
            pltpu.VMEM((len(blocks), 8, SLOTS), jnp.float32),
        ],
        compiler_params=pltpu.CompilerParams(vmem_limit_bytes=20 << 20),
        cost_estimate=pl.CostEstimate(
            flops=2 * EFFORT * pairs * width,
            bytes_accessed=2 * len(names) * HALF * width,
            transcendentals=0,
        ),
        name="pair_max",
    )(*(held[name] for name in names), before, *extra)


def unsort_kernel(got_ref, slot_ref, out_ref, row_ref):
    rows = slot_ref.shape[1]
    core, z, y, x = here()
    row_ref[...] = jnp.full(row_ref.shape, NONE, jnp.float32)
    for section in range(SECTIONS):
        half, turn = section // SIDE, section % SIDE
        owner = core if half == 0 else 1 - core
        found = []
        for step in STEPS.values():
            row = partner(owner, z, y, x, turn, -step.get("u", 0), -step.get("v", 0))
            found.append(got_ref[pl.ds(row + owner * 64, 1), :])
        row_ref[section : section + 1, :] = functools.reduce(jnp.maximum, found)
    columns = row_ref[...].T
    best = jnp.full((1, rows), NONE, jnp.float32)
    for section in range(SECTIONS):
        place = lax.broadcasted_iota(jnp.int32, (BOUND, rows), 0) + section * BOUND
        found = jnp.where(slot_ref[...] == place, columns[:BOUND, section : section + 1], NONE)
        best = jnp.maximum(best, jnp.max(found, 0, keepdims=True))
    out_ref[...] = best


def unsort(got, slot):
    vmem = pl.BlockSpec(memory_space=pltpu.VMEM)
    return pl.pallas_call(
        unsort_kernel,
        in_specs=[vmem] * 2,
        out_specs=vmem,
        out_shape=jax.ShapeDtypeStruct(slot.shape, jnp.float32),
        scratch_shapes=[pltpu.VMEM((LANES, LANES), jnp.float32)],
        name="unsort",
    )(got, slot)


def on_device(embeddings, cluster):
    mine, other, slot = sort_rows(embeddings, cluster.reshape(1, -1))

    def section(block, step):
        return block[step * BOUND : (step + 1) * BOUND]

    held = {}
    near = {step: take(section(mine, step), ring=-step) for step in (2, 1, 3)}
    far = {step: take(section(other, step), core=1, ring=-step) for step in (2, 1, 3, 0)}
    near[0] = section(mine, 0)
    held["0", "m"] = jnp.concatenate([near[step] for step in range(SIDE)], 0)
    held["0", "s"] = jnp.concatenate([far[step] for step in range(SIDE)], 0)
    for part in "ms":
        held["v1", part] = take(held["0", part], v=1)
        held["u1", part] = take(held["0", part], u=1)
        held["u3", part] = take(held["0", part], u=-1)
    held["v2", "m"] = take(held["v1", "m"], v=1)
    held["v2", "s"] = take(held["v1", "s"], v=1)
    held["u2", "m"] = take(held["u3", "m"], u=-1)
    held["u2", "s"] = take(held["u1", "s"], u=1)

    plan = (
        ([("0", "ms", "0", "lane")], []),
        ([("v1", "m", "0", "both")], []),
        ([("u1", "m", "0", "both")], [held["u3", "m"]]),
        ([("v1", "s", "0", "both"), ("u1", "s", "0", "both")], []),
        ([("u1", "ms", "v1", "both"), ("u3", "ms", "v1", "both")], []),
        ([("v2", "m", "0", "both", 0, 1), ("v2", "m", "u1", "both")], []),
        ([("u2", "m", "0", "lane", 0, 1), ("u2", "m", "v1", "both")], []),
        (
            [
                ("u2", "s", "0", "both"),
                ("u2", "s", "v1", "both"),
                ("v2", "m", "u2", "both", 0, 1),
            ],
            [],
        ),
        ([("v2", "s", near, "both") for near in ("0", "u1", "u2")], []),
    )
    best = jnp.full((len(BLOCKS), SLOTS), NONE, jnp.float32)
    for k, (products, extra) in enumerate(plan):
        best = pair_max(held, best, products, k + 1 == len(plan), extra)
    got = lax.all_to_all(best, AXES, 0, 0, tiled=True)
    return unsort(got, slot).reshape(-1)


def solution(mesh):
    in_specs = (P(AXES, None), P(AXES))
    return jax.shard_map(
        on_device, mesh=mesh, in_specs=in_specs, out_specs=P(AXES), check_vma=False
    )
```

```python
import functools

import jax
import jax.numpy as jnp
from jax import lax
from jax.experimental import pallas as pl
from jax.experimental.pallas import tpu as pltpu
from jax.sharding import PartitionSpec as P

AXES = ("group", "member")
SIDE = 4
CORES = 2
DEVICES = CORES * SIDE**3
BOUND = 96
HALF = SIDE * BOUND
SLOTS = CORES * HALF
TILE = 256
START = {"w": 0, "m": 0, "s": HALF}
STEPS = {
    "0": {"u": 0, "v": 0},
    "u1": {"u": 1},
    "u3": {"u": -1},
    "v1": {"v": 1},
    "u2": {"u": 2},
    "v2": {"v": 2},
}
BLOCKS = tuple(STEPS)
SECTIONS = 2 * SIDE
LANES = 128
EFFORT = 6
LOW = -8.0
NONE = -2.0


def place(device):
    return (device // 64, device // 16 % 4, device // 4 % 4, device % 4)


def device_at(core, z, y, x):
    return core * 64 + z % 4 * 16 + y % 4 * 4 + x % 4


def moved(device, core=0, ring=0, u=0, v=0):
    c, z, y, x = place(device)
    if c == 0:
        z, x, y = z + ring, x + u, y + v
    else:
        x, z, y = x + ring, z + u, y - v
    return device_at((c + core) % 2, z, y, x)


def take(block, **step):
    route = [(moved(device, **step), device) for device in range(DEVICES)]
    return lax.ppermute(block, AXES, route)


def here():
    member = lax.axis_index("member")
    return lax.axis_index("group"), member // 16, member // 4 % 4, member % 4


def partner(core, z, y, x, ring, u, v):
    ring = (jnp.where(core == 0, z, x) + ring) & 3
    u = (jnp.where(core == 0, x, z) + u) & 3
    y = (jnp.where(core == 0, y + v, y - v)) & 3
    return ring * jnp.where(core == 0, 16, 1) + u * jnp.where(core == 0, 1, 16) + y * 4


def sort_kernel(rows_ref, cluster_ref, mine_ref, other_ref, slot_ref):
    rows = rows_ref.shape[0]
    core, z, y, x = here()
    ring_mine, ring_other = jnp.where(core == 0, z, x), jnp.where(core == 0, x, z)
    before = lax.broadcasted_iota(jnp.int32, (rows, rows), 0) < lax.broadcasted_iota(
        jnp.int32, (rows, rows), 1
    )
    before = jnp.where(before, 1.0, 0.0).astype(jnp.bfloat16)
    cluster = cluster_ref[...]
    hits = cluster == lax.broadcasted_iota(jnp.int32, (8, rows), 0)
    hits = jnp.where(hits, 1.0, 0.0)
    counted = jnp.dot(hits.astype(jnp.bfloat16), before, preferred_element_type=jnp.float32)
    rank = jnp.sum(counted * hits, 0, keepdims=True).astype(jnp.int32)
    is_mine = cluster // 4 == core
    turn = (cluster + 4 - jnp.where(is_mine, ring_mine, ring_other)) % 4
    slot = (jnp.where(is_mine, 0, 4) + turn) * BOUND + rank
    slot_ref[...] = slot
    values = rows_ref[...].astype(jnp.float32)
    total = jnp.sum(values * values, 1, keepdims=True)
    normed = (values * lax.rsqrt(total + 1e-06)).astype(jnp.bfloat16)
    for start, out_ref in ((0, mine_ref), (HALF, other_ref)):
        picks = slot - start == lax.broadcasted_iota(jnp.int32, (HALF, rows), 0)
        picks = jnp.where(picks, 1.0, 0.0)
        used = jnp.max(picks, 1, keepdims=True)
        placed = jnp.dot(picks.astype(jnp.bfloat16), normed, preferred_element_type=jnp.float32)
        first = lax.broadcasted_iota(jnp.int32, (HALF, LANES), 1) == 0
        head = jnp.where(first & (used < 0.5), 2.0, placed[:, :LANES])
        out_ref[:, :LANES] = head.astype(jnp.bfloat16)
        out_ref[:, LANES:] = placed[:, LANES:].astype(jnp.bfloat16)


def sort_rows(embeddings, cluster):
    rows, width = embeddings.shape
    vmem = pl.BlockSpec(memory_space=pltpu.VMEM)
    return pl.pallas_call(
        sort_kernel,
        in_specs=[vmem, vmem],
        out_specs=[vmem] * 3,
        out_shape=[
            jax.ShapeDtypeStruct((HALF, width), jnp.bfloat16),
            jax.ShapeDtypeStruct((HALF, width), jnp.bfloat16),
            jax.ShapeDtypeStruct((1, rows), jnp.int32),
        ],
        compiler_params=pltpu.CompilerParams(vmem_limit_bytes=20 << 20),
        cost_estimate=pl.CostEstimate(
            flops=4 * rows * HALF * width, bytes_accessed=6 * rows * width, transcendentals=rows
        ),
        name="sort_rows",
    )(embeddings, cluster)


def empty(values):
    return jnp.where(values[:, :LANES].astype(jnp.float32) > 1.5, LOW, 0.0)


def pair_kernel(names, blocks, products, *refs):
    chunks = dict(zip(names, refs))
    before_ref = refs[len(names)]
    best_ref, fold_ref, lane_ref = refs[-3:]
    fold_blocks = {upper for upper, parts, lower, kind, *tiles in products if kind != "lane"}
    lane_blocks = {lower for upper, parts, lower, kind, *tiles in products if kind != "fold"}
    for block in fold_blocks:
        fold_ref[blocks.index(block)] = jnp.full(fold_ref.shape[1:], LOW, jnp.float32)
    for block in lane_blocks:
        lane_ref[blocks.index(block)] = jnp.full(lane_ref.shape[1:], LOW, jnp.float32)
    for upper, parts, lower, kind, *tiles in products:
        for tile in tiles or range(SLOTS // TILE):
            columns = slice(tile * TILE, (tile + 1) * TILE)
            if tile == 0:
                right = chunks[lower, "m"][:TILE, :]
            elif tile == 1:
                first, second = chunks[lower, "m"], chunks[lower, "s"]
                right = jnp.concatenate([first[TILE:, :], second[: TILE // 2, :]], 0)
            else:
                right = chunks[lower, "s"][TILE // 2 :, :]
            if kind != "lane":
                across = empty(right).T[:1, :]
            for part in parts:
                values = chunks[upper, part][...]
                rows = values.shape[0]
                scores = lax.dot_general(
                    values, right, (((1,), (1,)), ((), ())), preferred_element_type=jnp.float32
                )
                if upper == lower:
                    row = lax.broadcasted_iota(jnp.int32, scores.shape, 0) + START[part]
                    column = lax.broadcasted_iota(jnp.int32, scores.shape, 1) + tile * TILE
                    scores = jnp.where(row == column, LOW, scores)
                if kind != "fold":
                    at = blocks.index(lower)
                    down = scores + empty(values)[:, :1]
                    down = jnp.max(down.reshape(rows // 8, 8, TILE), 0)
                    lane_ref[at, :, columns] = jnp.maximum(lane_ref[at, :, columns], down)
                if kind != "lane":
                    at = (blocks.index(upper), slice(START[part], START[part] + rows))
                    over = scores + across
                    over = jnp.maximum(over[:, :LANES], over[:, LANES:])
                    fold_ref[at] = jnp.maximum(fold_ref[at], over)
    best = [before_ref[k : k + 1, :] for k in range(len(BLOCKS))]
    for block in blocks:
        at, k = blocks.index(block), BLOCKS.index(block)
        if block in fold_blocks:
            best[k] = jnp.maximum(best[k], jnp.max(fold_ref[at].T, 0, keepdims=True))
        if block in lane_blocks:
            best[k] = jnp.maximum(best[k], jnp.max(lane_ref[at], 0, keepdims=True))
    if best_ref.shape[0] == len(BLOCKS):
        best_ref[...] = jnp.concatenate(best, 0)
        return
    best_ref[...] = jnp.full(best_ref.shape, NONE, jnp.float32)
    core, z, y, x = here()
    for section in range(SECTIONS):
        half, turn = section // SIDE, section % SIDE
        for k, step in enumerate(STEPS.values()):
            row = partner(core, z, y, x, -turn, step.get("u", 0), step.get("v", 0))
            row += (core if half == 0 else 1 - core) * 64
            best_ref[pl.ds(row, 1), :BOUND] = best[k][:, section * BOUND : (section + 1) * BOUND]


def pair_max(held, before, products, last, extra):
    names, blocks = [], []
    for upper, parts, lower, kind, *tiles in products:
        names += [(upper, part) for part in parts]
        names += [(lower, "m"), (lower, "s")]
        blocks += [lower] * (kind != "fold") + [upper] * (kind != "lane")
    names, blocks = list(dict.fromkeys(names)), list(dict.fromkeys(blocks))
    vmem = pl.BlockSpec(memory_space=pltpu.VMEM)
    width = held[names[0]].shape[1]
    pairs = sum(
        held[upper, part].shape[0] * (TILE * len(tiles) if tiles else SLOTS)
        for upper, parts, lower, kind, *tiles in products
        for part in parts
    )
    shape = (DEVICES, LANES) if last else before.shape
    return pl.pallas_call(
        functools.partial(pair_kernel, names, blocks, products),
        in_specs=[vmem] * (len(names) + 1)
        + [pl.BlockSpec(memory_space=pl.ANY)] * len(extra),
        out_specs=vmem,
        out_shape=jax.ShapeDtypeStruct(shape, jnp.float32),
        scratch_shapes=[
            pltpu.VMEM((len(blocks), SLOTS, LANES), jnp.float32),
            pltpu.VMEM((len(blocks), 8, SLOTS), jnp.float32),
        ],
        compiler_params=pltpu.CompilerParams(vmem_limit_bytes=20 << 20),
        cost_estimate=pl.CostEstimate(
            flops=2 * EFFORT * pairs * width,
            bytes_accessed=2 * len(names) * HALF * width,
            transcendentals=0,
        ),
        name="pair_max",
    )(*(held[name] for name in names), before, *extra)


def unsort_kernel(got_ref, slot_ref, out_ref, row_ref):
    rows = slot_ref.shape[1]
    core, z, y, x = here()
    row_ref[...] = jnp.full(row_ref.shape, NONE, jnp.float32)
    for section in range(SECTIONS):
        half, turn = section // SIDE, section % SIDE
        owner = core if half == 0 else 1 - core
        found = []
        for step in STEPS.values():
            row = partner(owner, z, y, x, turn, -step.get("u", 0), -step.get("v", 0))
            found.append(got_ref[pl.ds(row + owner * 64, 1), :])
        row_ref[section : section + 1, :] = functools.reduce(jnp.maximum, found)
    columns = row_ref[...].T
    place = lax.broadcasted_iota(jnp.int32, (BOUND, rows), 0)
    best = jnp.full((BOUND, rows), NONE, jnp.float32)
    for section in range(SECTIONS):
        here_now = slot_ref[...] - section * BOUND == place
        best = jnp.where(here_now, columns[:BOUND, section : section + 1], best)
    out_ref[...] = jnp.max(best, 0, keepdims=True)


def unsort(got, slot):
    vmem = pl.BlockSpec(memory_space=pltpu.VMEM)
    return pl.pallas_call(
        unsort_kernel,
        in_specs=[vmem] * 2,
        out_specs=vmem,
        out_shape=jax.ShapeDtypeStruct(slot.shape, jnp.float32),
        scratch_shapes=[pltpu.VMEM((LANES, LANES), jnp.float32)],
        name="unsort",
    )(got, slot)


def on_device(embeddings, cluster):
    mine, other, slot = sort_rows(embeddings, cluster.reshape(1, -1))

    def section(block, step):
        return block[step * BOUND : (step + 1) * BOUND]

    held = {}
    near = {step: take(section(mine, step), ring=-step) for step in (2, 1, 3)}
    far = {step: take(section(other, step), core=1, ring=-step) for step in (2, 1, 3, 0)}
    near[0] = section(mine, 0)
    held["0", "m"] = jnp.concatenate([near[step] for step in range(SIDE)], 0)
    held["0", "s"] = jnp.concatenate([far[step] for step in range(SIDE)], 0)
    for part in "ms":
        held["v1", part] = take(held["0", part], v=1)
        held["u1", part] = take(held["0", part], u=1)
        held["u3", part] = take(held["0", part], u=-1)
    held["v2", "m"] = take(held["v1", "m"], v=1)
    held["v2", "s"] = take(held["v1", "s"], v=1)
    held["u2", "m"] = take(held["u3", "m"], u=-1)
    held["u2", "s"] = take(held["u1", "s"], u=1)

    plan = (
        ([("0", "ms", "0", "lane")], []),
        ([("v1", "m", "0", "both")], []),
        ([("u1", "m", "0", "both")], [held["u3", "m"]]),
        ([("v1", "s", "0", "both"), ("u1", "s", "0", "both")], []),
        ([("u1", "ms", "v1", "both"), ("u3", "ms", "v1", "both")], []),
        ([("v2", "m", "0", "both", 0, 1), ("v2", "m", "u1", "both")], []),
        ([("u2", "m", "0", "lane", 0, 1), ("u2", "m", "v1", "both")], []),
        (
            [
                ("u2", "s", "0", "both"),
                ("u2", "s", "v1", "both"),
                ("v2", "m", "u2", "both", 0, 1),
            ],
            [],
        ),
        ([("v2", "s", near, "both") for near in ("0", "u1", "u2")], []),
    )
    best = jnp.full((len(BLOCKS), SLOTS), NONE, jnp.float32)
    for k, (products, extra) in enumerate(plan):
        best = pair_max(held, best, products, k + 1 == len(plan), extra)
    got = lax.all_to_all(best, AXES, 0, 0, tiled=True)
    return unsort(got, slot).reshape(-1)


def solution(mesh):
    in_specs = (P(AXES, None), P(AXES))
    return jax.shard_map(
        on_device, mesh=mesh, in_specs=in_specs, out_specs=P(AXES), check_vma=False
    )
```
